128 devices in a mesh: mesh: 8 (over z, core), grid: 16 (over y, x).
Axes of the slice: x: 4, y: 4, z: 4, core: 2. Of those that a mesh axis runs over, the one named last changes fastest.
Arguments:
- mesh_latent: bfloat16 [65536, 512], P(('mesh', 'grid')), may hold values from -6 to 6
- grid_latent: bfloat16 [524288, 512], P(('mesh', 'grid')), may hold values from -6 to 6
- w_send: bfloat16 [512, 512], replicated, may hold values from -0.25 to 0.25
- w_grid: bfloat16 [512, 512], replicated, may hold values from -0.25 to 0.25
- w_agg: bfloat16 [512, 512], replicated, may hold values from -0.25 to 0.25
- w_out: bfloat16 [512, 512], replicated, may hold values from -0.25 to 0.25
- cotangent: bfloat16 [524288, 512], P(('mesh', 'grid')), may hold values from -6 to 6
- tile_mesh: int32 [6144], P(('mesh', 'grid')), may hold values from 0 to 511, as said below
- tile_grid: int32 [6144], P(('mesh', 'grid')), may hold values from 0 to 31, as said below
- tile_count: int32 [128], P(('mesh', 'grid')), may hold values from 24 to 48, as said below
- tile_mask: int32 [6144, 128, 128], P(('mesh', 'grid')), may hold values from 0 to 1
Outputs:
- decoded: bfloat16 [524288, 512], P(('mesh', 'grid'))
- grad_grid: bfloat16 [524288, 512], P(('mesh', 'grid'))
- grad_mesh: bfloat16 [65536, 512], P(('mesh', 'grid'))
- grad_send: float32 [512, 512], replicated
- grad_wgrid: float32 [512, 512], replicated
- grad_wagg: float32 [512, 512], replicated
- grad_wout: float32 [512, 512], replicated
The draws below stay inside these ranges and needn't reach their ends.
Inputs may be any that keep to these rules, and one draw needn't show every extreme that they name: `tile_mesh`: along the curve order: a tile's mesh block lies in the same index of mesh as its device, and within the blocks of that device or of the device just before or after it along grid; used slots come in order of grid block. `tile_grid`: unused slots hold 0. `tile_count`: some device uses all 48 slots.
All inputs are finite; a program needn't handle non-finite values.
Results may differ from the reference program's by a relative error of at most 0.0095.
Values may be sent and summed in bfloat16 or wider, within the bound.
A program may use at most 192 MiB of HBM per device.

```python
import jax
import jax.numpy as jnp
from jax import lax

L = 512
H = 512
BLOCK = 128
GB_DEV = 32
MB_DEV = 4
TILES_DEV = 48
GRID_NODES = 524288
MESH_NODES = 65536
N_GRID = 16
DEVICES = 128


def tile_counts(key):
    counts = jax.random.randint(jax.random.fold_in(key, 101), (DEVICES,), TILES_DEV // 2, TILES_DEV + 1)
    fullest = jax.random.randint(jax.random.fold_in(key, 102), (), 0, DEVICES)
    return jnp.where(jnp.arange(DEVICES) == fullest, TILES_DEV, counts).astype(jnp.int32)


def grid_blocks(key):
    counts = tile_counts(key)
    rows = jnp.arange(DEVICES * TILES_DEV)
    device = rows // TILES_DEV
    slot = rows % TILES_DEV
    used = counts[device]
    return jnp.where(slot < used, slot * GB_DEV // used, 0).astype(jnp.int32)


def draw_tile_count(key, part):
    return tile_counts(key)


def draw_tile_grid(key, part):
    return grid_blocks(key)


def draw_tile_mesh(key, part):
    blocks = grid_blocks(key)
    key = jax.random.fold_in(key, 7)
    rows = jnp.arange(DEVICES * TILES_DEV)
    device = rows // TILES_DEV
    slot = rows % TILES_DEV
    offset = jax.random.randint(key, (DEVICES * TILES_DEV,), -MB_DEV, MB_DEV + 1)
    offset = jnp.where(slot == 0, -MB_DEV, jnp.where(slot == 1, MB_DEV, offset))
    centre = device * MB_DEV + blocks * MB_DEV // GB_DEV
    lowest = device // N_GRID * N_GRID * MB_DEV
    highest = lowest + N_GRID * MB_DEV - 1
    return jnp.clip(centre + offset, lowest, highest).astype(jnp.int32)


def draw_tile_mask(key, part):
    key = jax.random.fold_in(key, 9)
    values = jax.random.randint(key, (DEVICES * TILES_DEV, BLOCK, BLOCK), 0, 4)
    return (values == 0).astype(jnp.int32)


def block_levels(rng, dims, cuts, low, largest):
    gain, own = 1.0, jax.random.fold_in(rng, 6)
    for dim, blocks in cuts:
        heights = jnp.exp(jax.random.uniform(jax.random.fold_in(own, dim), (blocks,), jnp.float32, low / len(cuts), largest / len(cuts)))
        gain = gain * jnp.repeat(heights, dims[dim] // blocks).reshape([-1 if axis == dim else 1 for axis in range(len(dims))])
    return gain


def centred(own_key, shape, scale, bound, pieces=(), held_as=jnp.bfloat16):
    drawn = jax.random.normal(own_key, shape, jnp.float32) * scale
    if len(pieces) > 0:
        drawn = block_levels(own_key, shape, pieces, -0.22, 0.18) * drawn
    return jnp.clip(drawn, min=-bound, max=bound).astype(held_as)


def setup_inputs(seed: int = 0) -> dict:
    arg_keys = jax.random.split(jax.random.key(seed), 12)
    mesh_latent = centred(arg_keys[0], (MESH_NODES, L), 1.0, 6.0, ((0, 128),))
    grid_latent = centred(arg_keys[1], (GRID_NODES, L), 1.0, 6.0, ((0, 128),))
    w_send = centred(arg_keys[2], (L, L), L ** -0.5, 0.25)
    w_grid = centred(arg_keys[3], (L, H), L ** -0.5, 0.25)
    w_agg = centred(arg_keys[4], (L, H), L ** -0.5, 0.25)
    w_out = centred(arg_keys[5], (H, L), H ** -0.5, 0.25)
    cotangent = centred(arg_keys[6], (GRID_NODES, L), 1.0, 6.0, ((0, 128),))
    tile_mesh = draw_tile_mesh(jax.random.fold_in(arg_keys[11], 71), 0)
    tile_grid = draw_tile_grid(jax.random.fold_in(arg_keys[11], 71), 0)
    tile_count = draw_tile_count(jax.random.fold_in(arg_keys[11], 71), 0)
    tile_mask = draw_tile_mask(jax.random.fold_in(arg_keys[11], 71), 0)
    return {"mesh_latent": mesh_latent, "grid_latent": grid_latent, "w_send": w_send, "w_grid": w_grid, "w_agg": w_agg, "w_out": w_out, "cotangent": cotangent, "tile_mesh": tile_mesh, "tile_grid": tile_grid, "tile_count": tile_count, "tile_mask": tile_mask}


edge_scale = 0.0625


def silu_slope(value):
    sig = jax.nn.sigmoid(value)
    return sig * (1.0 + value * (1.0 - sig))


def reference(mesh_latent, grid_latent, w_send, w_grid, w_agg, w_out, cotangent, tile_mesh, tile_grid, tile_count, tile_mask):
    ndevice = tile_count.shape[0]
    per_dev = tile_mesh.shape[0] // ndevice
    block = tile_mask.shape[1]
    width = mesh_latent.shape[1]
    grid_rows = grid_latent.shape[0] // ndevice
    sender_pre = jnp.dot(mesh_latent, w_send, preferred_element_type=jnp.float32)
    panels = jax.nn.silu(sender_pre).astype(jnp.bfloat16)
    masks = tile_mask.reshape(ndevice, per_dev, block, block)
    meshes = tile_mesh.reshape(ndevice, per_dev)
    grids = tile_grid.reshape(ndevice, per_dev)

    def device_agg(inputs):
        mesh_ids, grid_ids, mask_set, used = inputs

        def add_tile(slot, total):
            rows = lax.dynamic_slice_in_dim(panels, (mesh_ids[slot] * block).astype(jnp.int32), block, 0)
            term = jnp.dot(mask_set[slot].astype(jnp.bfloat16), rows, preferred_element_type=jnp.float32)
            term = jnp.where(slot < used, term, jnp.zeros_like(term))
            start = (grid_ids[slot] * block).astype(jnp.int32)
            old = lax.dynamic_slice_in_dim(total, start, block, 0)
            return lax.dynamic_update_slice_in_dim(total, old + term, start, 0)

        return lax.fori_loop(0, per_dev, add_tile, jnp.zeros((grid_rows, width), jnp.float32))

    agg_sum = lax.map(device_agg, (meshes, grids, masks, tile_count)).reshape(-1, width)
    agg = (agg_sum * edge_scale).astype(jnp.bfloat16)
    pre = jnp.dot(grid_latent, w_grid, preferred_element_type=jnp.float32) + jnp.dot(agg, w_agg, preferred_element_type=jnp.float32)
    hidden = jax.nn.silu(pre).astype(jnp.bfloat16)
    decoded = (grid_latent.astype(jnp.float32) + jnp.dot(hidden, w_out, preferred_element_type=jnp.float32)).astype(jnp.bfloat16)
    dhidden = jnp.dot(cotangent, w_out.T, preferred_element_type=jnp.float32)
    dpre = (dhidden * silu_slope(pre)).astype(jnp.bfloat16)
    grid_scale = grid_latent.shape[0] ** -0.5
    grad_wout = jnp.dot(hidden.T, cotangent, preferred_element_type=jnp.float32) * grid_scale
    grad_wgrid = jnp.dot(grid_latent.T, dpre, preferred_element_type=jnp.float32) * grid_scale
    grad_wagg = jnp.dot(agg.T, dpre, preferred_element_type=jnp.float32) * grid_scale
    dagg = jnp.dot(dpre, w_agg.T, preferred_element_type=jnp.float32).astype(jnp.bfloat16)
    grad_grid = (cotangent.astype(jnp.float32) + jnp.dot(dpre, w_grid.T, preferred_element_type=jnp.float32)).astype(jnp.bfloat16)

    def device_back(index, total):
        def add_tile(slot, inner):
            grid_start = ((index * (grid_rows // block) + grids[index, slot]) * block).astype(jnp.int32)
            rows = lax.dynamic_slice_in_dim(dagg, grid_start, block, 0)
            term = jnp.dot(masks[index, slot].T.astype(jnp.bfloat16), rows, preferred_element_type=jnp.float32)
            term = jnp.where(slot < tile_count[index], term, jnp.zeros_like(term))
            start = (meshes[index, slot] * block).astype(jnp.int32)
            old = lax.dynamic_slice_in_dim(inner, start, block, 0)
            return lax.dynamic_update_slice_in_dim(inner, old + term, start, 0)

        return lax.fori_loop(0, per_dev, add_tile, total)

    dpanels = lax.fori_loop(0, ndevice, device_back, jnp.zeros(panels.shape, jnp.float32))
    dsender = (dpanels * edge_scale * silu_slope(sender_pre)).astype(jnp.bfloat16)
    grad_mesh = jnp.dot(dsender, w_send.T, preferred_element_type=jnp.float32).astype(jnp.bfloat16)
    grad_send = jnp.dot(mesh_latent.T, dsender, preferred_element_type=jnp.float32) * (mesh_latent.shape[0] ** -0.5)
    return (decoded, grad_grid, grad_mesh, grad_send, grad_wgrid, grad_wagg, grad_wout)
```

```python
import functools

import jax
import jax.numpy as jnp
from jax import lax
from jax.experimental import pallas as pl
from jax.experimental.pallas import tpu as pltpu
from jax.sharding import PartitionSpec as P

edge_scale = 0.0625
MESH = pl.DeviceIdType.MESH
MIB = 1024 * 1024
CHUNK = 512
VMEM = pltpu.VMEM
NT = (((1,), (1,)), ((), ()))
TN = (((0,), (0,)), ((), ()))
f32 = jnp.float32
bf16 = jnp.bfloat16


def mm(a, b):
    return jnp.dot(a, b, preferred_element_type=f32)


def mm_nt(a, b):
    return lax.dot_general(a, b, NT, preferred_element_type=f32)


def mm_tn(a, b):
    return lax.dot_general(a, b, TN, preferred_element_type=f32)


def silu_parts(v):
    sig = 0.5 * jnp.tanh(0.5 * v) + 0.5
    act = v * sig
    return act, sig + act * (1.0 - sig)


def ring_ids(groups):
    row = lax.axis_index("mesh")
    col = lax.axis_index("grid")
    return (row, lax.rem(col + groups - 1, groups)), (row, lax.rem(col + 1, groups))


def halo_kernel(
    groups, mesh_ref, grid_ref, cot_ref, wg_ref, wo_ref, halo_ref, pre_ref, dhid_ref, send_sem, recv_sem
):
    left, right = ring_ids(groups)
    rows = mesh_ref.shape[0]
    barrier = pltpu.get_barrier_semaphore()
    for peer in (left, right):
        pl.semaphore_signal(barrier, inc=1, device_id=peer, device_id_type=MESH)
    pl.semaphore_wait(barrier, 2)
    copies = []
    for slot, peer in enumerate((right, left)):
        copies.append(
            pltpu.make_async_remote_copy(
                src_ref=mesh_ref,
                dst_ref=halo_ref.at[pl.ds(slot * rows, rows)],
                send_sem=send_sem.at[slot],
                recv_sem=recv_sem.at[slot],
                device_id=peer,
                device_id_type=MESH,
            )
        )
    for copy in copies:
        copy.start()

    def body(grid_blk, cot_blk, pre_blk, dhid_blk):
        pre_blk[...] = mm(grid_blk[...], wg_ref[...])
        dhid_blk[...] = mm_nt(cot_blk[...], wo_ref[...])

    width = grid_ref.shape[1]
    spec = pl.BlockSpec((CHUNK, width), lambda i: (i, 0))
    pltpu.emit_pipeline(
        body,
        grid=(grid_ref.shape[0] // CHUNK,),
        in_specs=[spec, spec],
        out_specs=[spec, spec],
    )(grid_ref, cot_ref, pre_ref, dhid_ref)
    for copy in copies:
        copy.wait()


def halo_call(groups, mesh_latent, grid_latent, cotangent, w_grid, w_out):
    rows, width = mesh_latent.shape
    grid_rows = grid_latent.shape[0]
    anyspec = pl.BlockSpec(memory_space=pl.ANY)
    vspec = pl.BlockSpec(memory_space=VMEM)
    return pl.pallas_call(
        functools.partial(halo_kernel, groups),
        name="halo",
        out_shape=[
            jax.ShapeDtypeStruct((2 * rows, width), bf16),
            jax.ShapeDtypeStruct((grid_rows, width), f32),
            jax.ShapeDtypeStruct((grid_rows, width), f32),
        ],
        in_specs=[anyspec, anyspec, anyspec, vspec, vspec],
        out_specs=[anyspec, anyspec, anyspec],
        scratch_shapes=[pltpu.SemaphoreType.DMA((2,)), pltpu.SemaphoreType.DMA((2,))],
        compiler_params=pltpu.CompilerParams(
            collective_id=0, has_side_effects=True, vmem_limit_bytes=32 * MIB
        ),
    )(mesh_latent, grid_latent, cotangent, w_grid, w_out)


def local_kernel(
    groups,
    send_scale,
    grid_scale,
    tmesh_ref,
    tgrid_ref,
    tcount_ref,
    mesh_ref,
    halo_ref,
    mask_ref,
    wsend_ref,
    wgrid_ref,
    wagg_ref,
    wout_ref,
    grid_ref,
    cot_ref,
    pre0_ref,
    dhid_ref,
    dec_ref,
    gg_ref,
    ds_ref,
    own_ref,
    packed_ref,
    panels,
    slope,
    mask_bf,
    agg_sum,
    dagg,
    source_sum,
    acc_out,
    acc_t,
):
    step = pl.program_id(0)
    slots, block, _ = mask_ref.shape
    mesh_rows, width = mesh_ref.shape
    first = (lax.axis_index("mesh") * groups + lax.axis_index("grid") - 1) * (mesh_rows // block)
    used = tcount_ref[0]

    def place(t):
        live = t < used
        m = jnp.where(live, tmesh_ref[t] - first, 0)
        g = jnp.where(live, tgrid_ref[t], 0)
        return pl.multiple_of(m * block, block), pl.multiple_of(g * block, block)

    def source(part):
        if part == 1:
            return mesh_ref[...]
        return halo_ref[pl.ds((part // 2) * mesh_rows, mesh_rows), :]

    @pl.when(step == 0)
    def _():
        for part in range(3):
            act, grad = silu_parts(mm(source(part), wsend_ref[...]))
            panels[pl.ds(part * mesh_rows, mesh_rows), :] = act.astype(bf16)
            slope[pl.ds(part * mesh_rows, mesh_rows), :] = grad
        agg_sum[...] = jnp.zeros_like(agg_sum)
        acc_out[...] = jnp.zeros_like(acc_out)
        acc_t[...] = jnp.zeros_like(acc_t)

        def group(outer, carry):
            for inner in range(8):
                t = outer * 8 + inner
                m, g = place(t)
                tile = jnp.where(t < used, mask_ref[t], 0).astype(f32).astype(bf16)
                mask_bf[t] = tile
                agg_sum[pl.ds(g, block), :] += mm(tile, panels[pl.ds(m, block), :])
            return carry

        lax.fori_loop(0, slots // 8, group, 0)

    rows = pl.ds(pl.multiple_of(step * CHUNK, CHUNK), CHUNK)
    agg = (agg_sum[rows, :] * edge_scale).astype(bf16)
    pre = pre0_ref[...] + mm(agg, wagg_ref[...])
    act, grad = silu_parts(pre)
    hidden = act.astype(bf16)
    dpre = (dhid_ref[...] * grad).astype(bf16)
    grid = grid_ref[...]
    cot = cot_ref[...]
    dec_ref[...] = (grid.astype(f32) + mm(hidden, wout_ref[...])).astype(bf16)
    gg_ref[...] = (cot.astype(f32) + mm_nt(dpre, wgrid_ref[...])).astype(bf16)
    dagg[rows, :] = mm_nt(dpre, wagg_ref[...]).astype(bf16)
    acc_out[...] += mm_tn(hidden, cot)
    dpre_t = dpre.T
    acc_t[:, :width] += mm(dpre_t, grid)
    acc_t[:, width:] += mm(dpre_t, agg)

    @pl.when(step == pl.num_programs(0) - 1)
    def _():
        source_sum[...] = jnp.zeros_like(source_sum)

        def group(outer, carry):
            for inner in range(8):
                t = outer * 8 + inner
                m, g = place(t)
                source_sum[pl.ds(m, block), :] += mm_tn(mask_bf[t], dagg[pl.ds(g, block), :])
            return carry

        lax.fori_loop(0, slots // 8, group, 0)
        local_send = jnp.zeros((width, width), f32)
        for part in range(3):
            part_rows = pl.ds(part * mesh_rows, mesh_rows)
            ds = source_sum[part_rows, :] * edge_scale * slope[part_rows, :]
            if part == 1:
                own_ref[...] = ds
            else:
                ds_ref[pl.ds((part // 2) * mesh_rows, mesh_rows), :] = ds.astype(bf16)
            local_send = local_send + mm_tn(source(part), ds.astype(bf16))
        wgrid_g = acc_t[:, :width].T
        wagg_g = acc_t[:, width:].T
        for index, (value, scale) in enumerate(
            (
                (local_send, send_scale),
                (wgrid_g, grid_scale),
                (wagg_g, grid_scale),
                (acc_out[...], grid_scale),
            )
        ):
            for c in range(width // 128):
                packed_ref[index, pl.ds(c * width, width), :] = (
                    value[:, c * 128 : (c + 1) * 128] * scale
                ).astype(bf16)


def local_call(
    groups,
    send_scale,
    grid_scale,
    tile_mesh,
    tile_grid,
    tile_count,
    mesh_latent,
    halo,
    tile_mask,
    w_send,
    w_grid,
    w_agg,
    w_out,
    grid_latent,
    cotangent,
    pre0,
    dhid,
):
    slots, block, _ = tile_mask.shape
    rows, width = mesh_latent.shape
    grid_rows = grid_latent.shape[0]
    once = pl.Buffered(buffer_count=1)

    def whole(shape):
        return pl.BlockSpec(shape, lambda i: (0,) * len(shape), pipeline_mode=once)

    def smem():
        return pl.BlockSpec(memory_space=pltpu.SMEM)

    chunked = pl.BlockSpec((CHUNK, width), lambda i: (i, 0))
    return pl.pallas_call(
        functools.partial(local_kernel, groups, send_scale, grid_scale),
        name="local",
        grid=(grid_rows // CHUNK,),
        out_shape=[
            jax.ShapeDtypeStruct((grid_rows, width), bf16),
            jax.ShapeDtypeStruct((grid_rows, width), bf16),
            jax.ShapeDtypeStruct((2 * rows, width), bf16),
            jax.ShapeDtypeStruct((rows, width), f32),
            jax.ShapeDtypeStruct((4, 4 * width, 128), bf16),
        ],
        in_specs=[
            smem(),
            smem(),
            smem(),
            whole((rows, width)),
            whole((2 * rows, width)),
            whole((slots, block, block)),
            whole((width, width)),
            whole((width, width)),
            whole((width, width)),
            whole((width, width)),
            chunked,
            chunked,
            chunked,
            chunked,
        ],
        out_specs=[
            chunked,
            chunked,
            whole((2 * rows, width)),
            whole((rows, width)),
            whole((4, 4 * width, 128)),
        ],
        scratch_shapes=[
            VMEM((3 * rows, width), bf16),
            VMEM((3 * rows, width), f32),
            VMEM((slots, block, block), bf16),
            VMEM((grid_rows, width), f32),
            VMEM((grid_rows, width), bf16),
            VMEM((3 * rows, width), f32),
            VMEM((width, width), f32),
            VMEM((width, 2 * width), f32),
        ],
        compiler_params=pltpu.CompilerParams(vmem_limit_bytes=58 * MIB),
    )(
        tile_mesh,
        tile_grid,
        tile_count,
        mesh_latent,
        halo,
        tile_mask,
        w_send,
        w_grid,
        w_agg,
        w_out,
        grid_latent,
        cotangent,
        pre0,
        dhid,
    )


ORDERS = (("y", "z", "x"), ("z", "y", "x"), ("y", "z", "x"), ("z", "y", "x"))


def sum_kernel(
    groups, packed_ref, ds_ref, own_ref, final_ref, dsend_ref, r0, r1, r2, r3, b0, b1, b2, a0, a1, a2, halo,
    send_sem, recv_sem, halo_send, halo_recv
):
    row = lax.axis_index("mesh")
    col = lax.axis_index("grid")
    core = lax.rem(row, 2)
    at = {"z": row // 2, "y": col // 4, "x": lax.rem(col, 4)}
    left, right = ring_ids(groups)
    sibling = (row + 1 - 2 * core, col)

    def peer(axis, d):
        to = lax.rem(at[axis] + d, 4)
        if axis == "z":
            return (to * 2 + core, col)
        if axis == "y":
            return (row, to * 4 + at["x"])
        return (row, at["y"] * 4 + to)

    barrier = pltpu.get_barrier_semaphore()
    others = [left, right, sibling] + [peer(axis, d) for axis in "xyz" for d in (1, 2, 3)]
    for other in others:
        pl.semaphore_signal(barrier, inc=1, device_id=other, device_id_type=MESH)
    pl.semaphore_wait(barrier, len(others))

    def remote(src, dst, sem, to):
        return pltpu.make_async_remote_copy(
            src_ref=src,
            dst_ref=dst,
            send_sem=send_sem.at[sem],
            recv_sem=recv_sem.at[sem],
            device_id=to,
            device_id_type=MESH,
        )

    count = packed_ref.shape[0]
    half = packed_ref.shape[1] // 2
    sizes = (half // 4, half // 16, half // 64)
    started = []

    def go(copy):
        copy.start()
        started.append(copy)
        return copy

    rows = own_ref.shape[0]
    stage0 = []
    for i in range(count):
        stage0.append(
            go(
                remote(
                    packed_ref.at[i, pl.ds(pl.multiple_of((1 - core) * half, half), half)],
                    r0.at[i],
                    i * 20,
                    sibling,
                )
            )
        )
    halos = []
    for slot, to in enumerate((left, right)):
        copy = pltpu.make_async_remote_copy(
            src_ref=ds_ref.at[pl.ds(slot * rows, rows)],
            dst_ref=halo.at[slot],
            send_sem=halo_send.at[slot],
            recv_sem=halo_recv.at[slot],
            device_id=to,
            device_id_type=MESH,
        )
        copy.start()
        halos.append(copy)

    received = (r1, r2, r3)
    outgoing = (b0, b1, b2)
    totals = (a0, a1, a2)

    def send_stage(i, stage):
        axis = ORDERS[i][stage]
        size = sizes[stage]
        copies = []
        for d in (1, 2, 3):
            to = lax.rem(at[axis] + d, 4)
            copies.append(
                go(
                    remote(
                        outgoing[stage].at[i, pl.ds(pl.multiple_of(to * size, size), size)],
                        received[stage].at[i, d - 1],
                        i * 20 + 1 + 3 * stage + d - 1,
                        peer(axis, d),
                    )
                )
            )
        return copies

    stage1 = []
    for i in range(count):
        stage0[i].wait_recv()
        mine = packed_ref[i, pl.ds(pl.multiple_of(core * half, half), half), :].astype(f32)
        total = mine + r0[i].astype(f32)
        a0[i] = total
        b0[i] = total.astype(bf16)
        stage1.append(send_stage(i, 0))
    stage_copies = stage1
    bases = [core * half for _ in range(count)]
    for stage in range(3):
        size = sizes[stage]
        following = []
        for i in range(count):
            axis = ORDERS[i][stage]
            for copy in stage_copies[i]:
                copy.wait_recv()
            offset = pl.multiple_of(at[axis] * size, size)
            total = totals[stage][i, pl.ds(offset, size), :]
            for d in range(3):
                total = total + received[stage][i, d].astype(f32)
            bases[i] = bases[i] + offset
            if stage < 2:
                totals[stage + 1][i] = total
                outgoing[stage + 1][i] = total.astype(bf16)
                following.append(send_stage(i, stage + 1))
            else:
                final_ref[i, pl.ds(pl.multiple_of(bases[i], 16), size), :] = total.astype(bf16)
        stage_copies = following

    def gather_stage(i, stage):
        axis = ORDERS[i][stage]
        size = sizes[stage]
        base = bases[i]
        for later in range(stage + 1, 3):
            base = base - at[ORDERS[i][later]] * sizes[later]
        window = final_ref.at[i, pl.ds(pl.multiple_of(base, size), size)]
        return [go(remote(window, window, i * 20 + 10 + 3 * stage + d - 1, peer(axis, d))) for d in (1, 2, 3)]

    gathers = [gather_stage(i, 2) for i in range(count)]
    for stage in (1, 0):
        following = []
        for i in range(count):
            for copy in gathers[i]:
                copy.wait_recv()
            following.append(gather_stage(i, stage))
        gathers = following
    last = []
    for i in range(count):
        for copy in gathers[i]:
            copy.wait_recv()
        window = final_ref.at[i, pl.ds(pl.multiple_of(core * half, half), half)]
        last.append(go(remote(window, window, i * 20 + 19, sibling)))

    for copy in halos:
        copy.wait()
    dsend_ref[...] = (own_ref[...] + halo[0].astype(f32) + halo[1].astype(f32)).astype(bf16)
    for copy in last:
        copy.wait_recv()
    for copy in started:
        copy.wait_send()


def sum_call(groups, packed, ds, own):
    rows, width = own.shape
    vspec = pl.BlockSpec(memory_space=VMEM)
    count, full, lanes = packed.shape
    half = full // 2
    sizes = (half // 4, half // 16, half // 64)
    return pl.pallas_call(
        functools.partial(sum_kernel, groups),
        name="sums",
        out_shape=[
            jax.ShapeDtypeStruct(packed.shape, bf16),
            jax.ShapeDtypeStruct((rows, width), bf16),
        ],
        in_specs=[vspec, vspec, vspec],
        out_specs=[vspec, vspec],
        scratch_shapes=[
            VMEM((count, half, lanes), bf16),
            VMEM((count, 3, sizes[0], lanes), bf16),
            VMEM((count, 3, sizes[1], lanes), bf16),
            VMEM((count, 3, sizes[2], lanes), bf16),
            VMEM((count, half, lanes), bf16),
            VMEM((count, sizes[0], lanes), bf16),
            VMEM((count, sizes[1], lanes), bf16),
            VMEM((count, half, lanes), f32),
            VMEM((count, sizes[0], lanes), f32),
            VMEM((count, sizes[1], lanes), f32),
            VMEM((2, rows, width), bf16),
            pltpu.SemaphoreType.DMA((20 * count,)),
            pltpu.SemaphoreType.DMA((20 * count,)),
            pltpu.SemaphoreType.DMA((2,)),
            pltpu.SemaphoreType.DMA((2,)),
        ],
        compiler_params=pltpu.CompilerParams(
            collective_id=1, has_side_effects=True, vmem_limit_bytes=40 * MIB
        ),
    )(packed, ds, own)


def finish_kernel(packed_ref, dsend_ref, wsend_ref, gm_ref, *grads):
    width = wsend_ref.shape[0]
    gm_ref[...] = mm_nt(dsend_ref[...], wsend_ref[...]).astype(bf16)
    for index, out in enumerate(grads):
        for c in range(width // 128):
            out[:, c * 128 : (c + 1) * 128] = packed_ref[index, pl.ds(c * width, width), :].astype(f32)


def finish_call(packed, dsend, w_send):
    width = w_send.shape[0]
    vspec = pl.BlockSpec(memory_space=VMEM)
    return pl.pallas_call(
        finish_kernel,
        name="finish",
        out_shape=[jax.ShapeDtypeStruct(dsend.shape, bf16)]
        + [jax.ShapeDtypeStruct((width, width), f32)] * 4,
        in_specs=[vspec] * 3,
        out_specs=[vspec] * 5,
        compiler_params=pltpu.CompilerParams(vmem_limit_bytes=32 * MIB),
    )(packed, dsend, w_send)


def per_device(
    mesh_latent,
    grid_latent,
    w_send,
    w_grid,
    w_agg,
    w_out,
    cotangent,
    tile_mesh,
    tile_grid,
    tile_count,
    tile_mask,
):
    groups = lax.axis_size("grid")
    devices_all = lax.axis_size("mesh") * groups
    send_scale = (mesh_latent.shape[0] * devices_all) ** (-0.5)
    grid_scale = (grid_latent.shape[0] * devices_all) ** (-0.5)
    halo, pre0, dhid = halo_call(groups, mesh_latent, grid_latent, cotangent, w_grid, w_out)
    decoded, grad_grid, ds, own, packed = local_call(
        groups,
        send_scale,
        grid_scale,
        tile_mesh,
        tile_grid,
        tile_count,
        mesh_latent,
        halo,
        tile_mask,
        w_send,
        w_grid,
        w_agg,
        w_out,
        grid_latent,
        cotangent,
        pre0,
        dhid,
    )
    final, dsend = sum_call(groups, packed, ds, own)
    grad_mesh, grad_send, grad_wgrid, grad_wagg, grad_wout = finish_call(final, dsend, w_send)
    return (decoded, grad_grid, grad_mesh, grad_send, grad_wgrid, grad_wagg, grad_wout)


def solution(mesh):
    both = ("mesh", "grid")
    return jax.shard_map(
        per_device,
        mesh=mesh,
        in_specs=(
            P(both, None),
            P(both, None),
            P(),
            P(),
            P(),
            P(),
            P(both, None),
            P(both),
            P(both),
            P(both),
            P(both, None, None),
        ),
        out_specs=(P(both, None), P(both, None), P(both, None), P(), P(), P(), P()),
        check_vma=False,
    )
```

```python
import functools

import jax
import jax.numpy as jnp
from jax import lax
from jax.experimental import pallas as pl
from jax.experimental.pallas import tpu as pltpu
from jax.sharding import PartitionSpec as P

edge_scale = 0.0625
MESH = pl.DeviceIdType.MESH
MIB = 1024 * 1024
CHUNK = 512
UNROLL = 8
VMEM = pltpu.VMEM
NT = (((1,), (1,)), ((), ()))
TN = (((0,), (0,)), ((), ()))
f32 = jnp.float32
bf16 = jnp.bfloat16
i32 = jnp.int32


def mm(a, b):
    return jnp.dot(a, b, preferred_element_type=f32)


def mm_nt(a, b):
    return lax.dot_general(a, b, NT, preferred_element_type=f32)


def mm_tn(a, b):
    return lax.dot_general(a, b, TN, preferred_element_type=f32)


def silu_parts(v):
    sig = 0.5 * jnp.tanh(0.5 * v) + 0.5
    act = v * sig
    return act, sig + act * (1.0 - sig)


def tile_tables(tile_mesh, tile_grid, tile_count, first, blocks, sources):
    slots = tile_mesh.shape[0]
    order = jnp.arange(slots, dtype=i32)
    live = order < tile_count[0]
    mesh_id = jnp.where(live, tile_mesh - first, sources)
    grid_id = jnp.where(live, tile_grid, blocks)
    same = (grid_id == jnp.roll(grid_id, 1)) & (order > 0)
    each = jnp.arange(blocks, dtype=i32)
    grid_last = jnp.sum((grid_id[None, :] <= each[:, None]).astype(i32), axis=1) - 1
    grid_has = jnp.any(grid_id[None, :] == each[:, None], axis=1)
    ahead = (mesh_id[None, :] < mesh_id[:, None]) | (
        (mesh_id[None, :] == mesh_id[:, None]) & (order[None, :] < order[:, None])
    )
    rank = jnp.sum(ahead.astype(i32), axis=1)
    pick = (rank[None, :] == order[:, None]).astype(i32)

    def ranked(values):
        return jnp.sum(pick * values[None, :], axis=1)

    sorted_mesh = ranked(mesh_id)
    source = jnp.arange(sources, dtype=i32)
    mesh_last = jnp.sum((mesh_id[None, :] <= source[:, None]).astype(i32), axis=1) - 1
    mesh_has = jnp.any(mesh_id[None, :] == source[:, None], axis=1)
    tables = {
        "fwd_mesh": jnp.where(live, mesh_id, 0),
        "fwd_same": same,
        "grid_last": jnp.where(grid_has, grid_last, slots),
        "bwd_slot": ranked(order),
        "bwd_grid": ranked(jnp.where(live, grid_id, 0)),
        "bwd_mesh": jnp.where(sorted_mesh < sources, sorted_mesh, 0),
        "bwd_same": (sorted_mesh == jnp.roll(sorted_mesh, 1)) & (order > 0),
        "mesh_last": jnp.where(mesh_has, mesh_last, slots),
    }
    places, at = {}, 0
    for name, value in tables.items():
        places[name] = at
        at += value.shape[0]
    return places, jnp.concatenate([value.astype(i32) for value in tables.values()])


ORDERS = (("y", "z", "x"), ("z", "y", "x"), ("y", "z", "x"), ("z", "y", "x"))
SEND, WGRID, WAGG, WOUT = 3, 1, 2, 0
SEMS = 20


def decoder_kernel(
    groups,
    places,
    send_scale,
    grid_scale,
    table,
    mesh_hbm,
    grid_hbm,
    cot_hbm,
    mask_hbm,
    wsend_hbm,
    wgrid_hbm,
    wagg_hbm,
    wout_hbm,
    dec_hbm,
    gg_hbm,
    gm_ref,
    final,
    grid_v,
    cot_v,
    pre_v,
    dpre_v,
    hidden_v,
    dagg_v,
    src_v,
    panels,
    slope,
    mask_i,
    mask_v,
    wsend_v,
    wgrid_v,
    wagg_v,
    wout_v,
    runs,
    total,
    acc_out,
    acc_t,
    ds_v,
    ds_in,
    packed,
    r0,
    r1,
    r2,
    r3,
    a1,
    b1,
    load_sem,
    chunk_sem,
    mask_sem,
    out_sem,
    halo_send,
    halo_recv,
    send_sem,
    recv_sem,
):
    slots, block, _ = mask_v.shape
    rows, width = mesh_hbm.shape
    grid_rows = grid_v.shape[0]
    chunks = grid_rows // CHUNK
    row = lax.axis_index("mesh")
    col = lax.axis_index("grid")
    core = lax.rem(row, 2)
    at = {"z": row // 2, "y": col // 4, "x": lax.rem(col, 4)}
    left = (row, lax.rem(col + groups - 1, groups))
    right = (row, lax.rem(col + 1, groups))
    sibling = (row + 1 - 2 * core, col)

    def peer(axis, d):
        to = lax.rem(at[axis] + d, 4)
        if axis == "z":
            return (to * 2 + core, col)
        if axis == "y":
            return (row, to * 4 + at["x"])
        return (row, at["y"] * 4 + to)

    def entry(name, index):
        return table[places[name] + index]

    barrier = pltpu.get_barrier_semaphore()
    others = [left, right, sibling] + [peer(axis, d) for axis in "xyz" for d in (1, 2, 3)]
    for other in others:
        pl.semaphore_signal(barrier, inc=1, device_id=other, device_id_type=MESH)
    loads = [
        pltpu.make_async_copy(src, dst, load_sem.at[k])
        for k, (src, dst) in enumerate(
            (
                (wgrid_hbm, wgrid_v),
                (wout_hbm, wout_v),
                (mesh_hbm, src_v.at[pl.ds(rows, rows)]),
                (wsend_hbm, wsend_v),
                (wagg_hbm, wagg_v),
            )
        )
    ]

    def chunk_loads(c):
        part = pl.ds(pl.multiple_of(c * CHUNK, CHUNK), CHUNK)
        return (
            pltpu.make_async_copy(grid_hbm.at[part], grid_v.at[part], chunk_sem.at[0, c]),
            pltpu.make_async_copy(cot_hbm.at[part], cot_v.at[part], chunk_sem.at[1, c]),
        )

    loads[0].start()
    loads[1].start()
    for copy in chunk_loads(0):
        copy.start()
    pl.semaphore_wait(barrier, len(others))
    halos = [
        pltpu.make_async_remote_copy(
            src_ref=mesh_hbm,
            dst_ref=src_v.at[pl.ds(2 * slot * rows, rows)],
            send_sem=halo_send.at[slot],
            recv_sem=halo_recv.at[slot],
            device_id=to,
            device_id_type=MESH,
        )
        for slot, to in enumerate((right, left))
    ]
    for copy in halos:
        copy.start()
    for c in range(1, chunks):
        for copy in chunk_loads(c):
            copy.start()
    for copy in loads[2:]:
        copy.start()
    quarter = mask_i.shape[0]
    masks = [
        pltpu.make_async_copy(mask_hbm.at[pl.ds(q * quarter, quarter)], mask_i, mask_sem)
        for q in range(slots // quarter)
    ]
    masks[0].start()

    loads[0].wait()
    loads[1].wait()

    def early(c, carry):
        for copy in chunk_loads(c):
            copy.wait()
        part = pl.ds(pl.multiple_of(c * CHUNK, CHUNK), CHUNK)
        pre_v[part, :] = mm(grid_v[part, :], wgrid_v[...])
        dpre_v[part, :] = mm_nt(cot_v[part, :], wout_v[...]).astype(bf16)
        return carry

    lax.fori_loop(0, chunks, early, 0)
    for copy in loads[2:]:
        copy.wait()

    per_part = rows // block

    def project(part):
        where = pl.ds(part * rows, rows)
        act, grad = silu_parts(mm(src_v[where, :], wsend_v[...]))
        blocks = pl.ds(part * per_part, per_part)
        panels[blocks] = act.astype(bf16).reshape(per_part, block, width)
        slope[blocks] = grad.reshape(per_part, block, width)

    project(1)
    for q, copy in enumerate(masks):
        copy.wait()

        def convert(k, carry, q=q):
            t = q * quarter + k
            mask_v[t] = mask_i[k].astype(f32).astype(bf16)
            return carry

        lax.fori_loop(0, quarter, convert, 0)
        if q + 1 < len(masks):
            masks[q + 1].start()
    acc_out[...] = jnp.zeros_like(acc_out)
    acc_t[...] = jnp.zeros_like(acc_t)
    total[...] = jnp.zeros_like(total)
    runs[slots] = jnp.zeros((block, width), bf16)
    for copy in halos:
        copy.wait()
    project(0)
    project(2)

    def forward(outer, carry):
        for inner in range(UNROLL):
            t = outer * UNROLL + inner
            keep = entry("fwd_same", t).astype(f32)
            value = total[...] * keep + mm(mask_v[t], panels[entry("fwd_mesh", t)])
            total[...] = value
            runs[t] = (value * edge_scale).astype(bf16)
        return carry

    lax.fori_loop(0, slots // UNROLL, forward, 0)

    def looked_up(last, index):
        return runs[entry(last, index)]

    per_chunk = CHUNK // block

    def node_mlp(c, carry):
        part = pl.ds(pl.multiple_of(c * CHUNK, CHUNK), CHUNK)
        agg = jnp.concatenate(
            [looked_up("grid_last", c * per_chunk + k) for k in range(per_chunk)], axis=0
        )
        act, grad = silu_parts(pre_v[part, :] + mm(agg, wagg_v[...]))
        hidden = act.astype(bf16)
        hidden_v[part, :] = hidden
        dpre = (dpre_v[part, :].astype(f32) * grad).astype(bf16)
        dpre_v[part, :] = dpre
        dagg = mm_nt(dpre, wagg_v[...]).astype(bf16)
        dagg_v[pl.ds(c * per_chunk, per_chunk)] = dagg.reshape(per_chunk, block, width)
        acc_out[...] += mm_tn(hidden, cot_v[part, :])
        dpre_t = dpre.T
        acc_t[:, :width] += mm(dpre_t, grid_v[part, :])
        acc_t[:, width:] += mm(dpre_t, agg)
        return carry

    lax.fori_loop(0, chunks, node_mlp, 0)

    half = packed.shape[1] // 2
    first_size, second_size = half // 4, half // 16
    mine = pl.multiple_of(core * half, half)
    theirs = pl.multiple_of((1 - core) * half, half)
    started = []

    def go(src, dst, sem, to):
        copy = pltpu.make_async_remote_copy(
            src_ref=src,
            dst_ref=dst,
            send_sem=send_sem.at[sem],
            recv_sem=recv_sem.at[sem],
            device_id=to,
            device_id_type=MESH,
        )
        copy.start()
        started.append(copy)
        return copy

    def fill(i, value, scale):
        for c in range(width // 128):
            packed[i, pl.ds(c * width, width), :] = (value[:, c * 128 : (c + 1) * 128] * scale).astype(bf16)

    def arrived(copies):
        for copy in copies:
            copy.wait_recv()

    def stream(i):
        axis_a, axis_b, axis_c = ORDERS[i]
        sem = i * SEMS
        copies = [go(packed.at[i, pl.ds(theirs, half)], r0.at[i], sem, sibling)]
        yield
        arrived(copies)
        off_a = pl.multiple_of(at[axis_a] * first_size, first_size)
        own = pl.multiple_of(mine + off_a, first_size)
        a1[i] = packed[i, pl.ds(own, first_size), :].astype(f32) + r0[i, pl.ds(off_a, first_size), :].astype(f32)
        r0[i] = (packed[i, pl.ds(mine, half), :].astype(f32) + r0[i].astype(f32)).astype(bf16)

        def scatter(source, target, axis, size, sem):
            return [
                go(
                    source.at[i, pl.ds(pl.multiple_of(lax.rem(at[axis] + d, 4) * size, size), size)],
                    target.at[i, d - 1],
                    sem + d,
                    peer(axis, d),
                )
                for d in (1, 2, 3)
            ]

        copies = scatter(r0, r1, axis_a, first_size, sem)
        yield
        arrived(copies)
        value = a1[i]
        for d in range(3):
            value = value + r1[i, d].astype(f32)
        a1[i] = value
        b1[i] = value.astype(bf16)
        copies = scatter(b1, r2, axis_b, second_size, sem + 3)
        yield
        arrived(copies)
        off_b = pl.multiple_of(at[axis_b] * second_size, second_size)
        value = a1[i, pl.ds(off_b, second_size), :]
        for d in range(3):
            value = value + r2[i, d].astype(f32)
        me = at[axis_c]
        r3[i, me] = value.astype(bf16)
        copies = [go(r3.at[i, me], r3.at[i, me], sem + 6 + d, peer(axis_c, d)) for d in (1, 2, 3)]
        yield
        arrived(copies)
        value = r3[i, 0].astype(f32)
        for k in range(1, 4):
            value = value + r3[i, k].astype(f32)
        place = pl.multiple_of(mine + off_a + off_b, second_size)
        final[i, pl.ds(place, second_size), :] = value.astype(bf16)

        def gather(place, size, axis, sem):
            window = final.at[i, pl.ds(place, size)]
            return [go(window, window, sem + d, peer(axis, d)) for d in (1, 2, 3)]

        copies = gather(place, second_size, axis_b, sem + 9)
        yield
        arrived(copies)
        copies = gather(own, first_size, axis_a, sem + 12)
        yield
        arrived(copies)
        window = final.at[i, pl.ds(mine, half)]
        copies = [go(window, window, sem + 16, sibling)]
        yield
        arrived(copies)

    streams = [stream(i) for i in range(4)]

    def advance(*which):
        for i in which:
            next(streams[i], None)

    fill(WOUT, acc_out[...], grid_scale)
    advance(WOUT)
    fill(WGRID, acc_t[:, :width].T, grid_scale)
    advance(WGRID)
    fill(WAGG, acc_t[:, width:].T, grid_scale)
    advance(WAGG)

    total[...] = jnp.zeros_like(total)

    def backward(outer, carry):
        for inner in range(UNROLL):
            r = outer * UNROLL + inner
            keep = entry("bwd_same", r).astype(f32)
            value = total[...] * keep + mm_tn(mask_v[entry("bwd_slot", r)], dagg_v[entry("bwd_grid", r)])
            total[...] = value
            runs[r] = (value * edge_scale * slope[entry("bwd_mesh", r)]).astype(bf16)
        return carry

    steps = slots // UNROLL
    lax.fori_loop(0, 3, backward, 0)
    advance(WOUT, WGRID, WAGG)
    lax.fori_loop(3, steps, backward, 0)
    for b in range(ds_v.shape[0] // block):
        ds_v[pl.ds(b * block, block), :] = looked_up("mesh_last", b)
    returns = [
        pltpu.make_async_remote_copy(
            src_ref=ds_v.at[pl.ds(2 * slot * rows, rows)],
            dst_ref=ds_in.at[slot],
            send_sem=halo_send.at[2 + slot],
            recv_sem=halo_recv.at[2 + slot],
            device_id=to,
            device_id_type=MESH,
        )
        for slot, to in enumerate((left, right))
    ]
    for copy in returns:
        copy.start()
    fill(SEND, mm_tn(src_v[...], ds_v[...]), send_scale)
    advance(SEND)

    def finish_chunk(c):
        part = pl.ds(c * CHUNK, CHUNK)
        dec = grid_v[part, :].astype(f32) + mm(hidden_v[part, :], wout_v[...])
        hidden_v[part, :] = dec.astype(bf16)
        out = pltpu.make_async_copy(hidden_v.at[part], dec_hbm.at[part], out_sem.at[0, c])
        out.start()
        gg = cot_v[part, :].astype(f32) + mm_nt(dpre_v[part, :], wgrid_v[...])
        dpre_v[part, :] = gg.astype(bf16)
        out_g = pltpu.make_async_copy(dpre_v.at[part], gg_hbm.at[part], out_sem.at[1, c])
        out_g.start()
        return [out, out_g]

    outs = []
    for c in range(chunks):
        outs += finish_chunk(c)
        if c == 1:
            advance(SEND)
        if c == 4:
            advance(WOUT, WGRID, WAGG)
    for _ in range(3):
        advance(SEND)
        advance(WOUT, WGRID, WAGG)
    for copy in returns:
        copy.wait()
    dsender = ds_v[pl.ds(rows, rows), :].astype(f32) + ds_in[0].astype(f32) + ds_in[1].astype(f32)
    gm_ref[...] = mm_nt(dsender.astype(bf16), wsend_v[...]).astype(bf16)
    for _ in range(8):
        advance(SEND, WOUT, WGRID, WAGG)
    for copy in outs:
        copy.wait()
    for copy in started:
        copy.wait_send()


def decoder_call(groups, places, send_scale, grid_scale, table, *arrays):
    mesh_latent, grid_latent, _, tile_mask = arrays[:4]
    slots, block, _ = tile_mask.shape
    rows, width = mesh_latent.shape
    grid_rows = grid_latent.shape[0]
    full = width * width // 128
    half = full // 2
    vspec = pl.BlockSpec(memory_space=VMEM)
    hspec = pl.BlockSpec(memory_space=pltpu.HBM)
    dma = pltpu.SemaphoreType.DMA
    weight = VMEM((width, width), bf16)
    node = VMEM((grid_rows, width), bf16)
    chunks = grid_rows // CHUNK
    return pl.pallas_call(
        functools.partial(decoder_kernel, groups, places, send_scale, grid_scale),
        name="decoder",
        out_shape=[
            jax.ShapeDtypeStruct((grid_rows, width), bf16),
            jax.ShapeDtypeStruct((grid_rows, width), bf16),
            jax.ShapeDtypeStruct((rows, width), bf16),
            jax.ShapeDtypeStruct((4, full, 128), bf16),
        ],
        in_specs=[pl.BlockSpec(memory_space=pltpu.SMEM)] + [hspec] * 8,
        out_specs=[hspec, hspec, vspec, vspec],
        scratch_shapes=[
            node,
            node,
            VMEM((grid_rows, width), f32),
            node,
            node,
            VMEM((grid_rows // block, block, width), bf16),
            VMEM((3 * rows, width), bf16),
            VMEM((3 * rows // block, block, width), bf16),
            VMEM((3 * rows // block, block, width), f32),
            VMEM((slots // 4, block, block), i32),
            VMEM((slots, block, block), bf16),
            weight,
            weight,
            weight,
            weight,
            VMEM((slots + 1, block, width), bf16),
            VMEM((block, width), f32),
            VMEM((width, width), f32),
            VMEM((width, 2 * width), f32),
            VMEM((3 * rows, width), bf16),
            VMEM((2, rows, width), bf16),
            VMEM((4, full, 128), bf16),
            VMEM((4, half, 128), bf16),
            VMEM((4, 3, half // 4, 128), bf16),
            VMEM((4, 3, half // 16, 128), bf16),
            VMEM((4, 4, half // 16, 128), bf16),
            VMEM((4, half // 4, 128), f32),
            VMEM((4, half // 4, 128), bf16),
            dma((5,)),
            dma((2, chunks)),
            dma,
            dma((2, chunks)),
            dma((4,)),
            dma((4,)),
            dma((4 * SEMS,)),
            dma((4 * SEMS,)),
        ],
        compiler_params=pltpu.CompilerParams(
            collective_id=0, has_side_effects=True, vmem_limit_bytes=61 * MIB
        ),
    )(table, *arrays)


def finish_kernel(packed_ref, *grads):
    width = grads[0].shape[0]
    for index, out in enumerate(grads):
        for c in range(width // 128):
            out[:, c * 128 : (c + 1) * 128] = packed_ref[index, pl.ds(c * width, width), :].astype(f32)


def finish_call(packed, width):
    vspec = pl.BlockSpec(memory_space=VMEM)
    return pl.pallas_call(
        finish_kernel,
        name="finish",
        out_shape=[jax.ShapeDtypeStruct((width, width), f32)] * 4,
        in_specs=[vspec],
        out_specs=[vspec] * 4,
        compiler_params=pltpu.CompilerParams(vmem_limit_bytes=32 * MIB),
    )(packed)


def per_device(
    mesh_latent,
    grid_latent,
    w_send,
    w_grid,
    w_agg,
    w_out,
    cotangent,
    tile_mesh,
    tile_grid,
    tile_count,
    tile_mask,
):
    block = tile_mask.shape[1]
    mesh_rows, width = mesh_latent.shape
    grid_rows = grid_latent.shape[0]
    groups = lax.axis_size("grid")
    devices_all = lax.axis_size("mesh") * groups
    send_scale = (mesh_rows * devices_all) ** (-0.5)
    grid_scale = (grid_rows * devices_all) ** (-0.5)
    mesh_blocks = mesh_rows // block
    first = (lax.axis_index("mesh") * groups + lax.axis_index("grid") - 1) * mesh_blocks
    places, table = tile_tables(
        tile_mesh, tile_grid, tile_count, first, grid_rows // block, 3 * mesh_blocks
    )
    decoded, grad_grid, grad_mesh, final = decoder_call(
        groups,
        places,
        send_scale,
        grid_scale,
        table,
        mesh_latent,
        grid_latent,
        cotangent,
        tile_mask,
        w_send,
        w_grid,
        w_agg,
        w_out,
    )
    grads = finish_call(final, width)
    return (decoded, grad_grid, grad_mesh, grads[SEND], grads[WGRID], grads[WAGG], grads[WOUT])


def solution(mesh):
    both = ("mesh", "grid")
    return jax.shard_map(
        per_device,
        mesh=mesh,
        in_specs=(
            P(both, None),
            P(both, None),
            P(),
            P(),
            P(),
            P(),
            P(both, None),
            P(both),
            P(both),
            P(both),
            P(both, None, None),
        ),
        out_specs=(P(both, None), P(both, None), P(both, None), P(), P(), P(), P()),
        check_vma=False,
    )
```

```python
import functools

import jax
import jax.numpy as jnp
from jax import lax
from jax.experimental import pallas as pl
from jax.experimental.pallas import tpu as pltpu
from jax.sharding import PartitionSpec as P

edge_scale = 0.0625
MESH = pl.DeviceIdType.MESH
MIB = 1024 * 1024
CHUNK = 512
UNROLL = 8
VMEM = pltpu.VMEM
NT = (((1,), (1,)), ((), ()))
TN = (((0,), (0,)), ((), ()))
f32 = jnp.float32
bf16 = jnp.bfloat16
i32 = jnp.int32


def mm(a, b):
    return jnp.dot(a, b, preferred_element_type=f32)


def mm_nt(a, b):
    return lax.dot_general(a, b, NT, preferred_element_type=f32)


def mm_tn(a, b):
    return lax.dot_general(a, b, TN, preferred_element_type=f32)


def silu_parts(v):
    sig = 0.5 * jnp.tanh(0.5 * v) + 0.5
    act = v * sig
    return act, sig + act * (1.0 - sig)


ROWS = {
    "fwd_mesh": 0,
    "fwd_same": 1,
    "grid_last": 2,
    "bwd_slot": 3,
    "bwd_grid": 4,
    "bwd_mesh": 5,
    "bwd_same": 6,
    "mesh_last": 7,
}


def tile_tables(tmesh, tgrid, tcount, first, blocks, sources, mesh_col, grid_col, out):
    slots = tmesh.shape[0]
    for t in range(slots):
        mesh_col[t : t + 1, :] = jnp.full((1, 128), tmesh[t], i32)
        grid_col[t : t + 1, :] = jnp.full((1, 128), tgrid[t], i32)
    shape = (slots, 128)
    sub = lax.broadcasted_iota(i32, shape, 0)
    lane = lax.broadcasted_iota(i32, shape, 1)
    live = sub < tcount[0]
    key = jnp.where(live, mesh_col[...] - first, sources)
    gid = jnp.where(live, grid_col[...], blocks)

    def down(mask, values):
        return jnp.sum(jnp.where(mask, values, 0), axis=0, keepdims=True)

    one = jnp.ones(shape, i32)
    diag = sub == lane
    later = lane[0:1, :] > 0
    key_row = down(diag, key)
    ahead = ((key_row < key) | ((key_row == key) & (lane < sub))) & (lane < slots)
    rank = jnp.sum(jnp.where(ahead, one, 0), axis=1, keepdims=True)
    pick = rank == lane
    sorted_key = down(pick, key)
    same_key = (sorted_key == down(rank == lane - 1, key)) & later
    grid_row = down(diag, gid)
    same_grid = (grid_row == down(sub == lane - 1, gid)) & later
    rows = {
        "fwd_mesh": down(diag & live, key),
        "fwd_same": same_grid.astype(i32),
        "grid_last": jnp.where(down(gid == lane, one) > 0, down(gid <= lane, one) - 1, slots),
        "bwd_slot": down(pick, sub),
        "bwd_grid": down(pick & live, gid),
        "bwd_mesh": jnp.where(sorted_key < sources, sorted_key, 0),
        "bwd_same": same_key.astype(i32),
        "mesh_last": jnp.where(down(key == lane, one) > 0, down(key <= lane, one) - 1, slots),
    }
    for name, value in rows.items():
        out[ROWS[name] : ROWS[name] + 1, :] = value


PLANE = tuple((dy, dz) for dy in range(4) for dz in range(4) if (dy, dz) != (0, 0))
SEND, WGRID, WAGG, WOUT = 3, 1, 2, 0
SEMS = 35
PIECES = 4


def decoder_kernel(
    groups,
    send_scale,
    grid_scale,
    tmesh,
    tgrid,
    tcount,
    mesh_hbm,
    grid_hbm,
    cot_hbm,
    mask_hbm,
    wsend_hbm,
    wgrid_hbm,
    wagg_hbm,
    wout_hbm,
    dec_hbm,
    gg_hbm,
    gm_hbm,
    final_hbm,
    grid_v,
    cot_v,
    pre_v,
    dpre_v,
    hidden_v,
    dagg_v,
    src_v,
    panels,
    slope,
    mask_i,
    mask_v,
    wsend_v,
    wgrid_v,
    wagg_v,
    wout_v,
    runs,
    total,
    acc_out,
    acc_t,
    ds_v,
    ds_in,
    packed,
    final,
    r0,
    r1,
    r3,
    gm_v,
    mesh_col,
    grid_col,
    table_v,
    table,
    load_sem,
    chunk_sem,
    mask_sem,
    table_sem,
    out_sem,
    end_sem,
    halo_send,
    halo_recv,
    send_sem,
    recv_sem,
):
    slots, block, _ = mask_v.shape
    rows, width = mesh_hbm.shape
    grid_rows = grid_v.shape[0]
    chunks = grid_rows // CHUNK
    row = lax.axis_index("mesh")
    col = lax.axis_index("grid")
    core = lax.rem(row, 2)
    at = {"z": row // 2, "y": col // 4, "x": lax.rem(col, 4)}
    left = (row, lax.rem(col + groups - 1, groups))
    right = (row, lax.rem(col + 1, groups))
    sibling = (row + 1 - 2 * core, col)

    def plane(dy, dz):
        to_y, to_z = lax.rem(at["y"] + dy, 4), lax.rem(at["z"] + dz, 4)
        return (to_z * 2 + core, to_y * 4 + at["x"]), to_y * 4 + to_z

    def along_x(d):
        return (row, at["y"] * 4 + lax.rem(at["x"] + d, 4))

    def entry(name, index):
        return table[ROWS[name], index]

    barrier = pltpu.get_barrier_semaphore()
    others = [left, right, sibling] + [along_x(d) for d in (1, 2, 3)] + [plane(*step)[0] for step in PLANE]
    for other in others:
        pl.semaphore_signal(barrier, inc=1, device_id=other, device_id_type=MESH)
    loads = [
        pltpu.make_async_copy(src, dst, load_sem.at[k])
        for k, (src, dst) in enumerate(
            (
                (wgrid_hbm, wgrid_v),
                (wout_hbm, wout_v),
                (mesh_hbm, src_v.at[pl.ds(rows, rows)]),
                (wsend_hbm, wsend_v),
                (wagg_hbm, wagg_v),
            )
        )
    ]

    def chunk_loads(c):
        part = pl.ds(pl.multiple_of(c * CHUNK, CHUNK), CHUNK)
        return (
            pltpu.make_async_copy(grid_hbm.at[part], grid_v.at[part], chunk_sem.at[0, c]),
            pltpu.make_async_copy(cot_hbm.at[part], cot_v.at[part], chunk_sem.at[1, c]),
        )

    quarter = mask_i.shape[1]
    masks = [
        pltpu.make_async_copy(mask_hbm.at[pl.ds(q * quarter, quarter)], mask_i.at[q % 2], mask_sem.at[q % 2])
        for q in range(slots // quarter)
    ]
    loads[0].start()
    loads[1].start()
    masks[0].start()
    for copy in chunk_loads(0):
        copy.start()
    pl.semaphore_wait(barrier, len(others))
    halos = [
        pltpu.make_async_remote_copy(
            src_ref=mesh_hbm,
            dst_ref=src_v.at[pl.ds(2 * slot * rows, rows)],
            send_sem=halo_send.at[slot],
            recv_sem=halo_recv.at[slot],
            device_id=to,
            device_id_type=MESH,
        )
        for slot, to in enumerate((right, left))
    ]
    for copy in halos:
        copy.start()
    masks[1].start()
    for c in range(1, chunks):
        for copy in chunk_loads(c):
            copy.start()
    for copy in loads[2:]:
        copy.start()
    loads[0].wait()
    loads[1].wait()

    def early(c, carry):
        for copy in chunk_loads(c):
            copy.wait()
        part = pl.ds(pl.multiple_of(c * CHUNK, CHUNK), CHUNK)
        pre_v[part, :] = mm(grid_v[part, :], wgrid_v[...])
        dpre_v[part, :] = mm_nt(cot_v[part, :], wout_v[...]).astype(bf16)
        return carry

    lax.fori_loop(0, chunks, early, 0)
    for copy in loads[2:]:
        copy.wait()

    per_part = rows // block

    def project(part):
        where = pl.ds(part * rows, rows)
        act, grad = silu_parts(mm(src_v[where, :], wsend_v[...]))
        blocks = pl.ds(part * per_part, per_part)
        panels[blocks] = act.astype(bf16).reshape(per_part, block, width)
        slope[blocks] = grad.reshape(per_part, block, width)

    project(1)
    per_grid = grid_rows // block
    first = (row * groups + col - 1) * per_part
    tile_tables(tmesh, tgrid, tcount, first, per_grid, 3 * per_part, mesh_col, grid_col, table_v)
    to_scalars = pltpu.make_async_copy(table_v, table, table_sem)
    to_scalars.start()
    for q, copy in enumerate(masks):
        copy.wait()

        def convert(k, carry, q=q):
            t = q * quarter + k
            mask_v[t] = mask_i[q % 2, k].astype(f32).astype(bf16)
            return carry

        lax.fori_loop(0, quarter, convert, 0)
        if q + 2 < len(masks):
            masks[q + 2].start()
    acc_out[...] = jnp.zeros_like(acc_out)
    acc_t[...] = jnp.zeros_like(acc_t)
    total[...] = jnp.zeros_like(total)
    runs[slots] = jnp.zeros((block, width), bf16)
    to_scalars.wait()
    for copy in halos:
        copy.wait()
    project(0)
    project(2)

    def forward(outer, carry):
        for inner in range(UNROLL):
            t = outer * UNROLL + inner
            keep = entry("fwd_same", t).astype(f32)
            value = total[...] * keep + mm(mask_v[t], panels[entry("fwd_mesh", t)])
            total[...] = value
            runs[t] = (value * edge_scale).astype(bf16)
        return carry

    lax.fori_loop(0, slots // UNROLL, forward, 0)

    def looked_up(last, index):
        return runs[entry(last, index)]

    per_chunk = CHUNK // block

    def agg_chunk(c):
        return jnp.concatenate([looked_up("grid_last", c * per_chunk + k) for k in range(per_chunk)], axis=0)

    def node_mlp(c, carry):
        part = pl.ds(pl.multiple_of(c * CHUNK, CHUNK), CHUNK)
        act, grad = silu_parts(pre_v[part, :] + mm(agg_chunk(c), wagg_v[...]))
        hidden = act.astype(bf16)
        hidden_v[part, :] = hidden
        dpre_v[part, :] = (dpre_v[part, :].astype(f32) * grad).astype(bf16)
        acc_out[...] += mm_tn(hidden, cot_v[part, :])
        return carry

    def input_grads(c, carry):
        part = pl.ds(pl.multiple_of(c * CHUNK, CHUNK), CHUNK)
        dpre_t = dpre_v[part, :].T
        acc_t[:, :width] += mm(dpre_t, grid_v[part, :])
        acc_t[:, width:] += mm(dpre_t, agg_chunk(c))
        return carry

    def agg_grads(c, carry):
        part = pl.ds(pl.multiple_of(c * CHUNK, CHUNK), CHUNK)
        dagg = mm_nt(dpre_v[part, :], wagg_v[...]).astype(bf16)
        dagg_v[pl.ds(c * per_chunk, per_chunk)] = dagg.reshape(per_chunk, block, width)
        return carry

    half = packed.shape[1] // 2
    size = half // 16
    place = pl.multiple_of((at["y"] * 4 + at["z"]) * size, size)
    mine = pl.multiple_of(core * half, half)
    theirs = pl.multiple_of((1 - core) * half, half)
    own = pl.multiple_of(mine + place, size)
    started = []

    def go(src, dst, sem, to):
        copy = pltpu.make_async_remote_copy(
            src_ref=src,
            dst_ref=dst,
            send_sem=send_sem.at[sem],
            recv_sem=recv_sem.at[sem],
            device_id=to,
            device_id_type=MESH,
        )
        copy.start()
        started.append(copy)
        return copy

    def fill(i, value, scale):
        for c in range(width // 128):
            packed[i, pl.ds(c * width, width), :] = (value[:, c * 128 : (c + 1) * 128] * scale).astype(bf16)

    def arrived(copies):
        for copy in copies:
            copy.wait_recv()

    def stream(i):
        sem = i * SEMS
        copies = [go(packed.at[i, pl.ds(theirs, half)], r0.at[i], sem, sibling)]
        yield
        arrived(copies)
        chunk = packed[i, pl.ds(own, size), :].astype(f32) + r0[i, pl.ds(place, size), :].astype(f32)
        r0[i] = (packed[i, pl.ds(mine, half), :].astype(f32) + r0[i].astype(f32)).astype(bf16)
        copies = []
        for k, step in enumerate(PLANE):
            to, index = plane(*step)
            window = pl.ds(pl.multiple_of(index * size, size), size)
            copies.append(go(r0.at[i, window], r1.at[i, k], sem + 1 + k, to))
        yield
        arrived(copies)
        for k in range(len(PLANE)):
            chunk = chunk + r1[i, k].astype(f32)
        me = at["x"]
        r3[i, me] = chunk.astype(bf16)
        copies = [go(r3.at[i, me], r3.at[i, me], sem + 15 + d, along_x(d)) for d in (1, 2, 3)]
        yield
        arrived(copies)
        value = r3[i, 0].astype(f32)
        for k in range(1, 4):
            value = value + r3[i, k].astype(f32)
        final[i, pl.ds(own, size), :] = value.astype(bf16)
        window = final.at[i, pl.ds(own, size)]
        copies = [go(window, window, sem + 19 + k, plane(*step)[0]) for k, step in enumerate(PLANE)]
        yield
        arrived(copies)
        window = final.at[i, pl.ds(mine, half)]
        copies = [go(window, window, sem + 34, sibling)]
        yield
        arrived(copies)
        out = pltpu.make_async_copy(final.at[i], final_hbm.at[i], end_sem.at[i])
        out.start()
        outs.append(out)

    outs = []
    streams = [stream(i) for i in range(4)]

    def advance(*which):
        for i in which:
            next(streams[i], None)

    lax.fori_loop(0, chunks, node_mlp, 0)
    fill(WOUT, acc_out[...], grid_scale)
    advance(WOUT)
    lax.fori_loop(0, chunks // 2, input_grads, 0)
    advance(WOUT)
    lax.fori_loop(chunks // 2, chunks, input_grads, 0)
    fill(WGRID, acc_t[:, :width].T, grid_scale)
    advance(WGRID)
    fill(WAGG, acc_t[:, width:].T, grid_scale)
    advance(WAGG)
    lax.fori_loop(0, chunks, agg_grads, 0)
    advance(WGRID, WAGG)

    total[...] = jnp.zeros_like(total)

    def backward(outer, carry):
        for inner in range(UNROLL):
            r = outer * UNROLL + inner
            keep = entry("bwd_same", r).astype(f32)
            value = total[...] * keep + mm_tn(mask_v[entry("bwd_slot", r)], dagg_v[entry("bwd_grid", r)])
            total[...] = value
            runs[r] = (value * edge_scale * slope[entry("bwd_mesh", r)]).astype(bf16)
        return carry

    lax.fori_loop(0, slots // UNROLL, backward, 0)
    advance(WOUT)
    for b in range(ds_v.shape[0] // block):
        ds_v[pl.ds(b * block, block), :] = looked_up("mesh_last", b)
    piece = rows // PIECES
    returns = [
        pltpu.make_async_remote_copy(
            src_ref=ds_v.at[pl.ds(2 * slot * rows + p * piece, piece)],
            dst_ref=ds_in.at[slot, pl.ds(p * piece, piece)],
            send_sem=halo_send.at[2 + 2 * p + slot],
            recv_sem=halo_recv.at[2 + 2 * p + slot],
            device_id=to,
            device_id_type=MESH,
        )
        for p in range(PIECES)
        for slot, to in enumerate((left, right))
    ]

    def give_back(p):
        for copy in returns[2 * p : 2 * p + 2]:
            copy.start()

    give_back(0)
    fill(SEND, mm_tn(src_v[...], ds_v[...]), send_scale)
    advance(SEND)

    def finish_chunk(c):
        part = pl.ds(c * CHUNK, CHUNK)
        dec = grid_v[part, :].astype(f32) + mm(hidden_v[part, :], wout_v[...])
        hidden_v[part, :] = dec.astype(bf16)
        out = pltpu.make_async_copy(hidden_v.at[part], dec_hbm.at[part], out_sem.at[0, c])
        out.start()
        gg = cot_v[part, :].astype(f32) + mm_nt(dpre_v[part, :], wgrid_v[...])
        dpre_v[part, :] = gg.astype(bf16)
        out_g = pltpu.make_async_copy(dpre_v.at[part], gg_hbm.at[part], out_sem.at[1, c])
        out_g.start()
        return [out, out_g]

    for c in range(chunks):
        outs += finish_chunk(c)
        if c == 1:
            advance(SEND)
        if c == 4:
            advance(WOUT)
            give_back(1)
    advance(WGRID, WAGG)
    give_back(2)
    advance(SEND)
    give_back(3)
    advance(WGRID, WAGG)
    advance(WOUT)
    advance(SEND)
    advance(WOUT)
    advance(WGRID, WAGG)
    for copy in returns:
        copy.wait()
    dsender = ds_v[pl.ds(rows, rows), :].astype(f32) + ds_in[0].astype(f32) + ds_in[1].astype(f32)
    gm_v[...] = mm_nt(dsender.astype(bf16), wsend_v[...]).astype(bf16)
    out = pltpu.make_async_copy(gm_v, gm_hbm, end_sem.at[4])
    out.start()
    outs.append(out)
    for _ in range(6):
        advance(SEND, WGRID, WAGG, WOUT)
    for copy in outs:
        copy.wait()
    for copy in started:
        copy.wait_send()


def decoder_call(groups, send_scale, grid_scale, *arrays):
    mesh_latent, grid_latent, _, tile_mask = arrays[3:7]
    slots, block, _ = tile_mask.shape
    rows, width = mesh_latent.shape
    grid_rows = grid_latent.shape[0]
    full = width * width // 128
    half = full // 2
    hspec = pl.BlockSpec(memory_space=pltpu.HBM)
    dma = pltpu.SemaphoreType.DMA
    weight = VMEM((width, width), bf16)
    node = VMEM((grid_rows, width), bf16)
    chunks = grid_rows // CHUNK
    return pl.pallas_call(
        functools.partial(decoder_kernel, groups, send_scale, grid_scale),
        name="decoder",
        out_shape=[
            jax.ShapeDtypeStruct((grid_rows, width), bf16),
            jax.ShapeDtypeStruct((grid_rows, width), bf16),
            jax.ShapeDtypeStruct((rows, width), bf16),
            jax.ShapeDtypeStruct((4, full, 128), bf16),
        ],
        in_specs=[pl.BlockSpec(memory_space=pltpu.SMEM)] * 3 + [hspec] * 8,
        out_specs=[hspec] * 4,
        scratch_shapes=[
            node,
            node,
            VMEM((grid_rows, width), f32),
            node,
            node,
            VMEM((grid_rows // block, block, width), bf16),
            VMEM((3 * rows, width), bf16),
            VMEM((3 * rows // block, block, width), bf16),
            VMEM((3 * rows // block, block, width), f32),
            VMEM((2, slots // 4, block, block), i32),
            VMEM((slots, block, block), bf16),
            weight,
            weight,
            weight,
            weight,
            VMEM((slots + 1, block, width), bf16),
            VMEM((block, width), f32),
            VMEM((width, width), f32),
            VMEM((width, 2 * width), f32),
            VMEM((3 * rows, width), bf16),
            VMEM((2, rows, width), bf16),
            VMEM((4, full, 128), bf16),
            VMEM((4, full, 128), bf16),
            VMEM((4, half, 128), bf16),
            VMEM((4, len(PLANE), half // 16, 128), bf16),
            VMEM((4, 4, half // 16, 128), bf16),
            VMEM((rows, width), bf16),
            VMEM((slots, 128), i32),
            VMEM((slots, 128), i32),
            VMEM((len(ROWS), 128), i32),
            pltpu.SMEM((len(ROWS), 128), i32),
            dma((5,)),
            dma((2, chunks)),
            dma((2,)),
            dma,
            dma((2, chunks)),
            dma((5,)),
            dma((2 + 2 * PIECES,)),
            dma((2 + 2 * PIECES,)),
            dma((4 * SEMS,)),
            dma((4 * SEMS,)),
        ],
        compiler_params=pltpu.CompilerParams(
            collective_id=0, has_side_effects=True, vmem_limit_bytes=61 * MIB
        ),
    )(*arrays)


def finish_kernel(dec_in, gg_in, gm_in, packed_hbm, dec, gg, gm, g0, g1, g2, g3, packed, grads, copy_sem, in_sem, out_sem):
    width = grads.shape[1]
    loads = [pltpu.make_async_copy(packed_hbm.at[i], packed.at[i], in_sem.at[i]) for i in range(4)]
    for load in loads:
        load.start()
    moves = [pltpu.make_async_copy(gm_in, gm, copy_sem.at[2 * PIECES])]
    piece = dec.shape[0] // PIECES
    for p in range(PIECES):
        part = pl.ds(p * piece, piece)
        moves.append(pltpu.make_async_copy(dec_in.at[part], dec.at[part], copy_sem.at[2 * p]))
        moves.append(pltpu.make_async_copy(gg_in.at[part], gg.at[part], copy_sem.at[2 * p + 1]))
    for move in moves:
        move.start()
    for index, out in enumerate((g0, g1, g2, g3)):
        loads[index].wait()
        for c in range(width // 128):
            grads[index, :, c * 128 : (c + 1) * 128] = packed[index, pl.ds(c * width, width), :].astype(f32)
        move = pltpu.make_async_copy(grads.at[index], out, out_sem.at[index])
        move.start()
        moves.append(move)
    for move in moves:
        move.wait()


def finish_call(decoded, grad_grid, grad_mesh, packed):
    width = grad_grid.shape[1]
    hspec = pl.BlockSpec(memory_space=pltpu.HBM)
    dma = pltpu.SemaphoreType.DMA
    return pl.pallas_call(
        finish_kernel,
        name="finish",
        out_shape=[jax.ShapeDtypeStruct(x.shape, x.dtype) for x in (decoded, grad_grid, grad_mesh)]
        + [jax.ShapeDtypeStruct((width, width), f32)] * 4,
        in_specs=[hspec] * 4,
        out_specs=[hspec] * 7,
        scratch_shapes=[
            VMEM(packed.shape, bf16),
            VMEM((4, width, width), f32),
            dma((2 * PIECES + 1,)),
            dma((4,)),
            dma((4,)),
        ],
        compiler_params=pltpu.CompilerParams(vmem_limit_bytes=32 * MIB),
    )(decoded, grad_grid, grad_mesh, packed)


def per_device(
    mesh_latent,
    grid_latent,
    w_send,
    w_grid,
    w_agg,
    w_out,
    cotangent,
    tile_mesh,
    tile_grid,
    tile_count,
    tile_mask,
):
    mesh_rows = mesh_latent.shape[0]
    grid_rows = grid_latent.shape[0]
    groups = lax.axis_size("grid")
    devices_all = lax.axis_size("mesh") * groups
    send_scale = (mesh_rows * devices_all) ** (-0.5)
    grid_scale = (grid_rows * devices_all) ** (-0.5)
    results = decoder_call(
        groups,
        send_scale,
        grid_scale,
        tile_mesh,
        tile_grid,
        tile_count,
        mesh_latent,
        grid_latent,
        cotangent,
        tile_mask,
        w_send,
        w_grid,
        w_agg,
        w_out,
    )
    decoded, grad_grid, grad_mesh, *grads = finish_call(*results)
    return (decoded, grad_grid, grad_mesh, grads[SEND], grads[WGRID], grads[WAGG], grads[WOUT])


def solution(mesh):
    both = ("mesh", "grid")
    return jax.shard_map(
        per_device,
        mesh=mesh,
        in_specs=(
            P(both, None),
            P(both, None),
            P(),
            P(),
            P(),
            P(),
            P(both, None),
            P(both),
            P(both),
            P(both),
            P(both, None, None),
        ),
        out_specs=(P(both, None), P(both, None), P(both, None), P(), P(), P(), P()),
        check_vma=False,
    )
```

```python
import functools

import jax
import jax.numpy as jnp
from jax import lax
from jax.experimental import pallas as pl
from jax.experimental.pallas import tpu as pltpu
from jax.sharding import PartitionSpec as P

edge_scale = 0.0625
MESH = pl.DeviceIdType.MESH
MIB = 1024 * 1024
CHUNK = 512
UNROLL = 8
VMEM = pltpu.VMEM
NT = (((1,), (1,)), ((), ()))
TN = (((0,), (0,)), ((), ()))
f32 = jnp.float32
bf16 = jnp.bfloat16
i32 = jnp.int32


def mm(a, b):
    return jnp.dot(a, b, preferred_element_type=f32)


def mm_nt(a, b):
    return lax.dot_general(a, b, NT, preferred_element_type=f32)


def mm_tn(a, b):
    return lax.dot_general(a, b, TN, preferred_element_type=f32)


def silu_parts(v):
    sig = 0.5 * jnp.tanh(0.5 * v) + 0.5
    act = v * sig
    return act, sig + act * (1.0 - sig)


ROWS = {
    "fwd_mesh": 0,
    "fwd_same": 1,
    "grid_last": 2,
    "bwd_slot": 3,
    "bwd_grid": 4,
    "bwd_mesh": 5,
    "bwd_same": 6,
    "mesh_last": 7,
}


def tile_tables(tmesh, tgrid, tcount, first, blocks, sources, mesh_col, grid_col, out):
    slots = tmesh.shape[0]
    for t in range(slots):
        mesh_col[t : t + 1, :] = jnp.full((1, 128), tmesh[t], i32)
        grid_col[t : t + 1, :] = jnp.full((1, 128), tgrid[t], i32)
    shape = (slots, 128)
    sub = lax.broadcasted_iota(i32, shape, 0)
    lane = lax.broadcasted_iota(i32, shape, 1)
    live = sub < tcount[0]
    key = jnp.where(live, mesh_col[...] - first, sources)
    gid = jnp.where(live, grid_col[...], blocks)

    def down(mask, values):
        return jnp.sum(jnp.where(mask, values, 0), axis=0, keepdims=True)

    one = jnp.ones(shape, i32)
    diag = sub == lane
    later = lane[0:1, :] > 0
    key_row = down(diag, key)
    ahead = ((key_row < key) | ((key_row == key) & (lane < sub))) & (lane < slots)
    rank = jnp.sum(jnp.where(ahead, one, 0), axis=1, keepdims=True)
    pick = rank == lane
    sorted_key = down(pick, key)
    same_key = (sorted_key == down(rank == lane - 1, key)) & later
    grid_row = down(diag, gid)
    same_grid = (grid_row == down(sub == lane - 1, gid)) & later
    rows = {
        "fwd_mesh": down(diag & live, key),
        "fwd_same": same_grid.astype(i32),
        "grid_last": jnp.where(down(gid == lane, one) > 0, down(gid <= lane, one) - 1, slots),
        "bwd_slot": down(pick, sub),
        "bwd_grid": down(pick & live, gid),
        "bwd_mesh": jnp.where(sorted_key < sources, sorted_key, 0),
        "bwd_same": same_key.astype(i32),
        "mesh_last": jnp.where(down(key == lane, one) > 0, down(key <= lane, one) - 1, slots),
    }
    for name, value in rows.items():
        out[ROWS[name] : ROWS[name] + 1, :] = value


PLANE = tuple((dy, dz) for dy in range(4) for dz in range(4) if (dy, dz) != (0, 0))
SEND, WGRID, WAGG, WOUT = 3, 1, 2, 0
SEMS = 35
ROUTES = {WOUT: ("z", "y"), WGRID: ("y", "z"), WAGG: ("z", "y"), SEND: "plane"}
PIECES = 4


def decoder_kernel(
    groups,
    send_scale,
    grid_scale,
    tmesh,
    tgrid,
    tcount,
    mesh_hbm,
    grid_hbm,
    cot_hbm,
    mask_hbm,
    wsend_hbm,
    wgrid_hbm,
    wagg_hbm,
    wout_hbm,
    dec_hbm,
    gg_hbm,
    gm_hbm,
    final_hbm,
    grid_v,
    cot_v,
    pre_v,
    dpre_v,
    hidden_v,
    dagg_v,
    src_v,
    panels,
    slope,
    mask_i,
    mask_v,
    wsend_v,
    wgrid_v,
    wagg_v,
    wout_v,
    runs,
    total,
    acc_out,
    acc_in,
    ds_v,
    ds_in,
    packed,
    final,
    r0,
    r1,
    r2,
    r3,
    a1,
    b1,
    mesh_col,
    grid_col,
    table_v,
    table,
    load_sem,
    chunk_sem,
    mask_sem,
    table_sem,
    out_sem,
    end_sem,
    halo_send,
    halo_recv,
    send_sem,
    recv_sem,
    near_sem,
):
    slots, block, _ = mask_v.shape
    rows, width = mesh_hbm.shape
    grid_rows = grid_v.shape[0]
    chunks = grid_rows // CHUNK
    row = lax.axis_index("mesh")
    col = lax.axis_index("grid")
    core = lax.rem(row, 2)
    at = {"z": row // 2, "y": col // 4, "x": lax.rem(col, 4)}
    left = (row, lax.rem(col + groups - 1, groups))
    right = (row, lax.rem(col + 1, groups))
    sibling = (row + 1 - 2 * core, col)

    def plane(dy, dz):
        to_y, to_z = lax.rem(at["y"] + dy, 4), lax.rem(at["z"] + dz, 4)
        return (to_z * 2 + core, to_y * 4 + at["x"]), to_y * 4 + to_z

    def along_x(d):
        return (row, at["y"] * 4 + lax.rem(at["x"] + d, 4))

    def tell_near(stage):
        for other in near:
            pl.semaphore_signal(near_sem.at[stage], inc=1, device_id=other, device_id_type=MESH)

    def hear_near(stage):
        pl.semaphore_wait(near_sem.at[stage], len(near))

    def entry(name, index):
        return table[ROWS[name], index]

    barrier = pltpu.get_barrier_semaphore()
    near = [along_x(1), along_x(3)] + [plane(*step)[0] for step in ((1, 0), (3, 0), (0, 1), (0, 3))]
    others = [left, right, sibling] + near
    for other in others:
        pl.semaphore_signal(barrier, inc=1, device_id=other, device_id_type=MESH)
    loads = [
        pltpu.make_async_copy(src, dst, load_sem.at[k])
        for k, (src, dst) in enumerate(
            (
                (wgrid_hbm, wgrid_v),
                (wout_hbm, wout_v),
                (mesh_hbm, src_v.at[pl.ds(rows, rows)]),
                (wsend_hbm, wsend_v),
                (wagg_hbm, wagg_v),
            )
        )
    ]

    def chunk_loads(c):
        part = pl.ds(pl.multiple_of(c * CHUNK, CHUNK), CHUNK)
        return (
            pltpu.make_async_copy(grid_hbm.at[part], grid_v.at[part], chunk_sem.at[0, c]),
            pltpu.make_async_copy(cot_hbm.at[part], cot_v.at[part], chunk_sem.at[1, c]),
        )

    quarter = mask_i.shape[1]
    masks = [
        pltpu.make_async_copy(mask_hbm.at[pl.ds(q * quarter, quarter)], mask_i.at[q % 2], mask_sem.at[q % 2])
        for q in range(slots // quarter)
    ]
    loads[0].start()
    loads[1].start()
    masks[0].start()
    for copy in chunk_loads(0):
        copy.start()
    pl.semaphore_wait(barrier, len(others))
    halos = [
        pltpu.make_async_remote_copy(
            src_ref=mesh_hbm,
            dst_ref=src_v.at[pl.ds(2 * slot * rows, rows)],
            send_sem=halo_send.at[slot],
            recv_sem=halo_recv.at[slot],
            device_id=to,
            device_id_type=MESH,
        )
        for slot, to in enumerate((right, left))
    ]
    for copy in halos:
        copy.start()
    tell_near(0)
    masks[1].start()
    for c in range(1, chunks):
        for copy in chunk_loads(c):
            copy.start()
    for copy in loads[2:]:
        copy.start()
    loads[0].wait()
    loads[1].wait()

    def early(c, carry):
        for copy in chunk_loads(c):
            copy.wait()
        part = pl.ds(pl.multiple_of(c * CHUNK, CHUNK), CHUNK)
        pre_v[part, :] = mm(grid_v[part, :], wgrid_v[...])
        dpre_v[part, :] = mm_nt(cot_v[part, :], wout_v[...]).astype(bf16)
        return carry

    lax.fori_loop(0, chunks, early, 0)
    for copy in loads[2:]:
        copy.wait()

    per_part = rows // block

    def project(part):
        where = pl.ds(part * rows, rows)
        act, grad = silu_parts(mm(src_v[where, :], wsend_v[...]))
        blocks = pl.ds(part * per_part, per_part)
        panels[blocks] = act.astype(bf16).reshape(per_part, block, width)
        slope[blocks] = grad.reshape(per_part, block, width)

    project(1)
    hear_near(0)
    tell_near(1)
    per_grid = grid_rows // block
    first = (row * groups + col - 1) * per_part
    tile_tables(tmesh, tgrid, tcount, first, per_grid, 3 * per_part, mesh_col, grid_col, table_v)
    to_scalars = pltpu.make_async_copy(table_v, table, table_sem)
    to_scalars.start()
    for q, copy in enumerate(masks):
        copy.wait()

        def convert(k, carry, q=q):
            t = q * quarter + k
            mask_v[t] = mask_i[q % 2, k].astype(f32).astype(bf16)
            return carry

        lax.fori_loop(0, quarter, convert, 0)
        if q + 2 < len(masks):
            masks[q + 2].start()
    hear_near(1)
    tell_near(2)
    acc_out[...] = jnp.zeros_like(acc_out)
    acc_in[...] = jnp.zeros_like(acc_in)
    total[...] = jnp.zeros_like(total)
    runs[slots] = jnp.zeros((block, width), bf16)
    to_scalars.wait()
    for copy in halos:
        copy.wait()
    project(0)
    project(2)
    hear_near(2)

    def forward(outer, carry):
        for inner in range(UNROLL):
            t = outer * UNROLL + inner
            keep = entry("fwd_same", t).astype(f32)
            value = total[...] * keep + mm(mask_v[t], panels[entry("fwd_mesh", t)])
            total[...] = value
            runs[t] = (value * edge_scale).astype(bf16)
        return carry

    lax.fori_loop(0, slots // UNROLL, forward, 0)

    def looked_up(last, index):
        return runs[entry(last, index)]

    per_chunk = CHUNK // block

    def agg_chunk(c):
        return jnp.concatenate([looked_up("grid_last", c * per_chunk + k) for k in range(per_chunk)], axis=0)

    def node_mlp(c, carry):
        part = pl.ds(pl.multiple_of(c * CHUNK, CHUNK), CHUNK)
        agg = agg_chunk(c)
        act, grad = silu_parts(pre_v[part, :] + mm(agg, wagg_v[...]))
        hidden = act.astype(bf16)
        hidden_v[part, :] = hidden
        dpre = (dpre_v[part, :].astype(f32) * grad).astype(bf16)
        dpre_v[part, :] = dpre
        acc_out[...] += mm_tn(hidden, cot_v[part, :])
        acc_in[:, :width] += mm_tn(grid_v[part, :], dpre)
        acc_in[:, width:] += mm_tn(agg, dpre)
        dagg = mm_nt(dpre, wagg_v[...]).astype(bf16)
        dagg_v[pl.ds(c * per_chunk, per_chunk)] = dagg.reshape(per_chunk, block, width)
        return carry

    lax.fori_loop(0, chunks, node_mlp, 0, unroll=2)

    half = packed.shape[1] // 2
    size = half // 16
    place = pl.multiple_of((at["y"] * 4 + at["z"]) * size, size)
    mine = pl.multiple_of(core * half, half)
    theirs = pl.multiple_of((1 - core) * half, half)
    own = pl.multiple_of(mine + place, size)
    started = []

    def go(src, dst, sem, to):
        copy = pltpu.make_async_remote_copy(
            src_ref=src,
            dst_ref=dst,
            send_sem=send_sem.at[sem],
            recv_sem=recv_sem.at[sem],
            device_id=to,
            device_id_type=MESH,
        )
        copy.start()
        started.append(copy)
        return copy

    def fill(i, value, scale):
        for c in range(width // 128):
            packed[i, pl.ds(c * width, width), :] = (value[:, c * 128 : (c + 1) * 128] * scale).astype(bf16)

    def arrived(copies):
        for copy in copies:
            copy.wait_recv()

    def stream(i):
        return plane_stream(i) if ROUTES[i] == "plane" else axes_stream(i)

    def along(axis, d):
        return plane(d, 0)[0] if axis == "y" else plane(0, d)[0]

    def meet(i, chunk, sem):
        me = at["x"]
        r3[i, me] = chunk.astype(bf16)
        return [go(r3.at[i, me], r3.at[i, me], sem + d - 1, along_x(d)) for d in (1, 2, 3)]

    def met(i, where):
        value = r3[i, 0].astype(f32)
        for k in range(1, 4):
            value = value + r3[i, k].astype(f32)
        final[i, pl.ds(where, size), :] = value.astype(bf16)

    def finished(i, sem):
        window = final.at[i, pl.ds(mine, half)]
        return [go(window, window, sem, sibling)]

    def store(i):
        out = pltpu.make_async_copy(final.at[i], final_hbm.at[i], end_sem.at[i])
        out.start()
        outs.append(out)

    def axes_stream(i):
        sem = i * SEMS
        axis_a, axis_b = ROUTES[i]
        wide = 4 * size
        copies = [go(packed.at[i, pl.ds(theirs, half)], r0.at[i], sem, sibling)]
        yield
        arrived(copies)
        off_a = pl.multiple_of(at[axis_a] * wide, wide)
        off_b = pl.multiple_of(at[axis_b] * size, size)
        base = pl.multiple_of(mine + off_a, wide)
        band = packed[i, pl.ds(base, wide), :].astype(f32) + r0[i, pl.ds(off_a, wide), :].astype(f32)
        r0[i] = (packed[i, pl.ds(mine, half), :].astype(f32) + r0[i].astype(f32)).astype(bf16)
        a1[i] = band
        copies = []
        for d in (1, 2, 3):
            window = pl.ds(pl.multiple_of(lax.rem(at[axis_a] + d, 4) * wide, wide), wide)
            slot = r2.at[i, d - 1]
            copies.append(go(r0.at[i, window], slot, sem + d, along(axis_a, d)))
        yield
        arrived(copies)
        band = a1[i]
        for d in range(3):
            band = band + r2[i, d].astype(f32)
        a1[i] = band
        b1[i] = band.astype(bf16)
        copies = []
        for d in (1, 2, 3):
            window = pl.ds(pl.multiple_of(lax.rem(at[axis_b] + d, 4) * size, size), size)
            copies.append(go(b1.at[i, window], r1.at[i, 11 + d], sem + 3 + d, along(axis_b, d)))
        yield
        arrived(copies)
        chunk = a1[i, pl.ds(off_b, size), :]
        for d in (1, 2, 3):
            chunk = chunk + r1[i, 11 + d].astype(f32)
        copies = meet(i, chunk, sem + 7)
        yield
        arrived(copies)
        here = pl.multiple_of(base + off_b, size)
        met(i, here)
        window = final.at[i, pl.ds(here, size)]
        copies = [go(window, window, sem + 9 + d, along(axis_b, d)) for d in (1, 2, 3)]
        yield
        arrived(copies)
        window = final.at[i, pl.ds(base, wide)]
        copies = [go(window, window, sem + 12 + d, along(axis_a, d)) for d in (1, 2, 3)]
        yield
        arrived(copies)
        copies = finished(i, sem + 34)
        yield
        arrived(copies)
        store(i)

    def plane_stream(i):
        sem = i * SEMS
        copies = [go(packed.at[i, pl.ds(theirs, half)], r0.at[i], sem, sibling)]
        yield
        arrived(copies)
        chunk = packed[i, pl.ds(own, size), :].astype(f32) + r0[i, pl.ds(place, size), :].astype(f32)
        r0[i] = (packed[i, pl.ds(mine, half), :].astype(f32) + r0[i].astype(f32)).astype(bf16)
        copies = []
        for k, step in enumerate(PLANE):
            to, index = plane(*step)
            window = pl.ds(pl.multiple_of(index * size, size), size)
            copies.append(go(r0.at[i, window], r1.at[i, k], sem + 1 + k, to))
        yield
        arrived(copies)
        for k in range(len(PLANE)):
            chunk = chunk + r1[i, k].astype(f32)
        copies = meet(i, chunk, sem + 16)
        yield
        arrived(copies)
        met(i, own)
        window = final.at[i, pl.ds(own, size)]
        copies = [go(window, window, sem + 19 + k, plane(*step)[0]) for k, step in enumerate(PLANE)]
        yield
        arrived(copies)
        copies = finished(i, sem + 34)
        yield
        arrived(copies)
        store(i)

    outs = []
    streams = [stream(i) for i in range(4)]

    def advance(*which):
        for i in which:
            next(streams[i], None)

    fill(WOUT, acc_out[...], grid_scale)
    advance(WOUT)
    fill(WGRID, acc_in[:, :width], grid_scale)
    advance(WGRID)
    fill(WAGG, acc_in[:, width:], grid_scale)
    advance(WAGG)

    total[...] = jnp.zeros_like(total)

    def backward(outer, carry):
        for inner in range(UNROLL):
            r = outer * UNROLL + inner
            keep = entry("bwd_same", r).astype(f32)
            value = total[...] * keep + mm_tn(mask_v[entry("bwd_slot", r)], dagg_v[entry("bwd_grid", r)])
            total[...] = value
            runs[r] = (value * edge_scale * slope[entry("bwd_mesh", r)]).astype(bf16)
        return carry

    for first_step, which in enumerate((WOUT, WGRID, WAGG)):
        lax.fori_loop(first_step, first_step + 1, backward, 0)
        advance(which)
    lax.fori_loop(3, slots // UNROLL, backward, 0)
    for b in range(ds_v.shape[0] // block):
        ds_v[pl.ds(b * block, block), :] = looked_up("mesh_last", b)
    piece = rows // PIECES
    returns = [
        pltpu.make_async_remote_copy(
            src_ref=ds_v.at[pl.ds(2 * slot * rows + p * piece, piece)],
            dst_ref=ds_in.at[slot, pl.ds(p * piece, piece)],
            send_sem=halo_send.at[2 + 2 * p + slot],
            recv_sem=halo_recv.at[2 + 2 * p + slot],
            device_id=to,
            device_id_type=MESH,
        )
        for p in range(PIECES)
        for slot, to in enumerate((left, right))
    ]

    def give_back(p):
        for copy in returns[2 * p : 2 * p + 2]:
            copy.start()

    give_back(0)
    fill(SEND, mm_tn(src_v[...], ds_v[...]), send_scale)
    advance(SEND)

    def finish_chunk(c):
        part = pl.ds(c * CHUNK, CHUNK)
        dec = grid_v[part, :].astype(f32) + mm(hidden_v[part, :], wout_v[...])
        hidden_v[part, :] = dec.astype(bf16)
        out = pltpu.make_async_copy(hidden_v.at[part], dec_hbm.at[part], out_sem.at[0, c])
        out.start()
        gg = cot_v[part, :].astype(f32) + mm_nt(dpre_v[part, :], wgrid_v[...])
        dpre_v[part, :] = gg.astype(bf16)
        out_g = pltpu.make_async_copy(dpre_v.at[part], gg_hbm.at[part], out_sem.at[1, c])
        out_g.start()
        return [out, out_g]

    for c in range(chunks):
        outs += finish_chunk(c)
        if c == 1:
            advance(SEND)
        if c == 2:
            advance(WOUT, WGRID, WAGG)
        if c == 3:
            give_back(1)
    advance(WOUT, WGRID, WAGG)
    advance(WOUT, WGRID, WAGG)
    give_back(2)
    advance(SEND)
    advance(WOUT, WGRID, WAGG)
    give_back(3)
    advance(SEND)
    advance(WOUT, WGRID, WAGG)
    advance(SEND)
    for copy in returns:
        copy.wait()
    dsender = ds_v[pl.ds(rows, rows), :].astype(f32) + ds_in[0].astype(f32) + ds_in[1].astype(f32)
    ds_in[0] = mm_nt(dsender.astype(bf16), wsend_v[...]).astype(bf16)
    out = pltpu.make_async_copy(ds_in.at[0], gm_hbm, end_sem.at[4])
    out.start()
    outs.append(out)
    for _ in range(6):
        advance(SEND, WGRID, WAGG, WOUT)
    for copy in outs:
        copy.wait()
    for copy in started:
        copy.wait_send()


def decoder_call(groups, send_scale, grid_scale, *arrays):
    mesh_latent, grid_latent, _, tile_mask = arrays[3:7]
    slots, block, _ = tile_mask.shape
    rows, width = mesh_latent.shape
    grid_rows = grid_latent.shape[0]
    full = width * width // 128
    half = full // 2
    hspec = pl.BlockSpec(memory_space=pltpu.HBM)
    dma = pltpu.SemaphoreType.DMA
    weight = VMEM((width, width), bf16)
    node = VMEM((grid_rows, width), bf16)
    chunks = grid_rows // CHUNK
    return pl.pallas_call(
        functools.partial(decoder_kernel, groups, send_scale, grid_scale),
        name="decoder",
        out_shape=[
            jax.ShapeDtypeStruct((grid_rows, width), bf16),
            jax.ShapeDtypeStruct((grid_rows, width), bf16),
            jax.ShapeDtypeStruct((rows, width), bf16),
            jax.ShapeDtypeStruct((4, full, 128), bf16),
        ],
        in_specs=[pl.BlockSpec(memory_space=pltpu.SMEM)] * 3 + [hspec] * 8,
        out_specs=[hspec] * 4,
        scratch_shapes=[
            node,
            node,
            VMEM((grid_rows, width), f32),
            node,
            node,
            VMEM((grid_rows // block, block, width), bf16),
            VMEM((3 * rows, width), bf16),
            VMEM((3 * rows // block, block, width), bf16),
            VMEM((3 * rows // block, block, width), f32),
            VMEM((2, slots // 8, block, block), i32),
            VMEM((slots, block, block), bf16),
            weight,
            weight,
            weight,
            weight,
            VMEM((slots + 1, block, width), bf16),
            VMEM((block, width), f32),
            VMEM((width, width), f32),
            VMEM((width, 2 * width), f32),
            VMEM((3 * rows, width), bf16),
            VMEM((2, rows, width), bf16),
            VMEM((4, full, 128), bf16),
            VMEM((4, full, 128), bf16),
            VMEM((4, half, 128), bf16),
            VMEM((4, len(PLANE), half // 16, 128), bf16),
            VMEM((4, 3, half // 4, 128), bf16),
            VMEM((4, 4, half // 16, 128), bf16),
            VMEM((4, half // 4, 128), f32),
            VMEM((4, half // 4, 128), bf16),
            VMEM((slots, 128), i32),
            VMEM((slots, 128), i32),
            VMEM((len(ROWS), 128), i32),
            pltpu.SMEM((len(ROWS), 128), i32),
            dma((5,)),
            dma((2, chunks)),
            dma((2,)),
            dma,
            dma((2, chunks)),
            dma((5,)),
            dma((2 + 2 * PIECES,)),
            dma((2 + 2 * PIECES,)),
            dma((4 * SEMS,)),
            dma((4 * SEMS,)),
            pltpu.SemaphoreType.REGULAR((3,)),
        ],
        compiler_params=pltpu.CompilerParams(
            collective_id=0, has_side_effects=True, vmem_limit_bytes=62 * MIB
        ),
    )(*arrays)


def finish_kernel(dec_in, gg_in, gm_in, packed_hbm, dec, gg, gm, g0, g1, g2, g3, packed, grads, copy_sem, in_sem, out_sem):
    width = grads.shape[1]
    loads = [pltpu.make_async_copy(packed_hbm.at[i], packed.at[i], in_sem.at[i]) for i in range(4)]
    for load in loads:
        load.start()
    moves = [pltpu.make_async_copy(gm_in, gm, copy_sem.at[2 * PIECES])]
    piece = dec.shape[0] // PIECES
    for p in range(PIECES):
        part = pl.ds(p * piece, piece)
        moves.append(pltpu.make_async_copy(dec_in.at[part], dec.at[part], copy_sem.at[2 * p]))
        moves.append(pltpu.make_async_copy(gg_in.at[part], gg.at[part], copy_sem.at[2 * p + 1]))
    for move in moves:
        move.start()
    for index, out in enumerate((g0, g1, g2, g3)):
        loads[index].wait()
        for c in range(width // 128):
            grads[index, :, c * 128 : (c + 1) * 128] = packed[index, pl.ds(c * width, width), :].astype(f32)
        move = pltpu.make_async_copy(grads.at[index], out, out_sem.at[index])
        move.start()
        moves.append(move)
    for move in moves:
        move.wait()


def finish_call(decoded, grad_grid, grad_mesh, packed):
    width = grad_grid.shape[1]
    hspec = pl.BlockSpec(memory_space=pltpu.HBM)
    dma = pltpu.SemaphoreType.DMA
    return pl.pallas_call(
        finish_kernel,
        name="finish",
        out_shape=[jax.ShapeDtypeStruct(x.shape, x.dtype) for x in (decoded, grad_grid, grad_mesh)]
        + [jax.ShapeDtypeStruct((width, width), f32)] * 4,
        in_specs=[hspec] * 4,
        out_specs=[hspec] * 7,
        scratch_shapes=[
            VMEM(packed.shape, bf16),
            VMEM((4, width, width), f32),
            dma((2 * PIECES + 1,)),
            dma((4,)),
            dma((4,)),
        ],
        compiler_params=pltpu.CompilerParams(vmem_limit_bytes=62 * MIB),
    )(decoded, grad_grid, grad_mesh, packed)


def per_device(
    mesh_latent,
    grid_latent,
    w_send,
    w_grid,
    w_agg,
    w_out,
    cotangent,
    tile_mesh,
    tile_grid,
    tile_count,
    tile_mask,
):
    mesh_rows = mesh_latent.shape[0]
    grid_rows = grid_latent.shape[0]
    groups = lax.axis_size("grid")
    devices_all = lax.axis_size("mesh") * groups
    send_scale = (mesh_rows * devices_all) ** (-0.5)
    grid_scale = (grid_rows * devices_all) ** (-0.5)
    results = decoder_call(
        groups,
        send_scale,
        grid_scale,
        tile_mesh,
        tile_grid,
        tile_count,
        mesh_latent,
        grid_latent,
        cotangent,
        tile_mask,
        w_send,
        w_grid,
        w_agg,
        w_out,
    )
    decoded, grad_grid, grad_mesh, *grads = finish_call(*results)
    return (decoded, grad_grid, grad_mesh, grads[SEND], grads[WGRID], grads[WAGG], grads[WOUT])


def solution(mesh):
    both = ("mesh", "grid")
    return jax.shard_map(
        per_device,
        mesh=mesh,
        in_specs=(
            P(both, None),
            P(both, None),
            P(),
            P(),
            P(),
            P(),
            P(both, None),
            P(both),
            P(both),
            P(both),
            P(both, None, None),
        ),
        out_specs=(P(both, None), P(both, None), P(both, None), P(), P(), P(), P()),
        check_vma=False,
    )
```
